128 devices in a mesh: pair: 16 (over x, z), virt: 8 (over y, core).
Axes of the slice: x: 4, y: 4, z: 4, core: 2. Of those that a mesh axis runs over, the one named last changes fastest.
Arguments:
- lambda_blocks: float32 [32, 1920, 1920], P('pair', 'virt'), may hold values from -1 to 1
- amplitudes: float32 [32, 1920, 1920], P('pair', 'virt'), may hold values from -1 to 1
- pair_list: int32 [32, 2], replicated, may hold values from 0 to 199, as said below
Outputs:
- density_virt: float32 [1920, 1920], P('virt', 'pair')
- density_occ: float32 [200, 200], replicated
The draws below stay inside these ranges and needn't reach their ends.
Inputs may be any that keep to these rules, and one draw needn't show every extreme that they name: `pair_list`: column 0 holds an occupied index below 200, reaching 199; column 1 holds one below 8; pairs may repeat.
All inputs are finite; a program needn't handle non-finite values.
Results may differ from the reference program's by a relative error of at most 0.00013.
Values sent between devices are 32-bit elements; how exact they have to be, the bound alone decides.
A program may use at most 256 MiB of HBM per device.

```python
import jax
import jax.numpy as jnp
from jax import lax

V = 1920
OCC = 200
NP = 32
KSET = 8


def draw_pair_list(key, part):
    key = jax.random.fold_in(key, 5)
    key_first, key_second, key_spot = jax.random.split(key, 3)
    first = jax.random.randint(key_first, (NP,), 0, OCC)
    spot = jax.random.randint(key_spot, (), 0, NP)
    first = jnp.where(jnp.arange(NP) == spot, OCC - 1, first)
    second = jax.random.randint(key_second, (NP,), 0, KSET)
    return jnp.stack([first, second], 1).astype(jnp.int32)


def block_scale(key, shape, shards, low, top_value):
    factor_of = 1.0
    for axis_at, shards_of in shards:
        heights = jax.random.uniform(jax.random.fold_in(jax.random.fold_in(key, 6), axis_at), (shards_of,), jnp.float32, low / len(shards), top_value / len(shards))
        factor_of = factor_of * jnp.repeat(jnp.exp(heights), shape[axis_at] // shards_of).reshape((-1,) + (1,) * (len(shape) - 1 - axis_at))
    return factor_of


def noise(rng, dims, deviation, limit, cuts=(), held_as=jnp.bfloat16):
    loudness = block_scale(rng, dims, cuts, -0.22, 0.18) if cuts else 1.0
    array = jax.random.normal(rng, dims, jnp.float32) * deviation * loudness
    return jnp.minimum(jnp.maximum(array, -limit), limit).astype(held_as)


def setup_inputs(seed: int = 0) -> dict:
    seeds = jax.random.split(jax.random.key(seed), 4)
    return {
        "lambda_blocks": noise(seeds[0], (NP, V, V), ((NP * V) ** -0.25), 1.0, ((0, 16), (1, 8)), jnp.float32),
        "amplitudes": noise(seeds[1], (NP, V, V), ((NP * V) ** -0.25), 1.0, ((0, 16), (1, 8)), jnp.float32),
        "pair_list": draw_pair_list(jax.random.fold_in(seeds[3], 71), 0),
    }


def reference(lambda_blocks, amplitudes, pair_list):
    density_virt = jnp.einsum('pac,pbc->ab', lambda_blocks, amplitudes, precision=lax.Precision.HIGHEST)
    intersection = jnp.einsum('pac,qac->pq', lambda_blocks, amplitudes, precision=lax.Precision.HIGHEST)
    first = pair_list[:, 0]
    second = pair_list[:, 1]
    one_hot = (first[:, None] == jnp.arange(OCC, dtype=jnp.int32)[None, :]).astype(jnp.float32)
    same_k = (second[:, None] == second[None, :]).astype(jnp.float32)
    inner = jnp.dot(same_k * intersection, one_hot, precision=lax.Precision.HIGHEST)
    density_occ = -jnp.dot(one_hot.T, inner, precision=lax.Precision.HIGHEST)
    return density_virt, density_occ
```

```python
import jax
import jax.numpy as jnp
from jax import lax
from jax.experimental import pallas as pl
from jax.experimental.pallas import tpu as pltpu
from jax.sharding import PartitionSpec as P

OCC = 200
NP = 32
ROWS = 240
PAD = 256
V = 1920
KC = 640
KPARTS = V // KC
STEPS = 2 * KPARTS
MESH = pl.DeviceIdType.MESH
F32 = jnp.float32
BF16 = jnp.bfloat16


class Copy:
    def __init__(self, *variants):
        self.variants = variants

    def _each(self, act):
        for cond, make in self.variants:
            if cond is None:
                act(make())
            else:

                @pl.when(cond)
                def _(make=make):
                    act(make())

    def start(self):
        self._each(lambda c: c.start())

    def wait_send(self):
        self._each(lambda c: c.wait_send())

    def wait_recv(self):
        self._each(lambda c: c.wait_recv())

    def wait(self):
        self._each(lambda c: c.wait())


class Sems:
    def __init__(self, send, recv):
        self.send, self.recv, self.n = send, recv, 0

    def take(self):
        self.n += 1
        return self.send.at[self.n - 1], self.recv.at[self.n - 1]


def split(v):
    hi = v.astype(BF16)
    return hi, (v - hi.astype(F32)).astype(BF16)


NT = (((1,), (1,)), ((), ()))


def dot_nt(a, b):
    return lax.dot_general(a, b, NT, preferred_element_type=F32)


N_SEMS = 128


def kernel(
    l_ref, t_ref, out_ref, inter_ref,
    lraw, traw, lcat, tcat, acc, lx, tz, lz, tx, gram,
    ro1, ro2, rp1, rp2, so, sp, fo, fp, yq, fin, ix, iz, iy, ic,
    send, recv, local,
):
    pair, virt = lax.axis_index("pair"), lax.axis_index("virt")
    x, z = lax.div(pair, 4), lax.rem(pair, 4)
    y, c = lax.div(virt, 2), lax.rem(virt, 2)
    sems = Sems(send, recv)

    def ring(a):
        return lax.rem(a + 4, 4)

    def dev(xx, zz, yy, cc):
        return (xx * 4 + zz, yy * 2 + cc)

    def at_x(d):
        return dev(ring(x + d), z, y, c)

    def at_z(d):
        return dev(x, ring(z + d), y, c)

    def at_y(d):
        return dev(x, z, ring(y + d), c)

    other = dev(x, z, y, 1 - c)
    y_l = y + 1 - 2 * lax.rem(y, 2)
    y_t = 3 - y
    to_l, to_t = dev(x, z, y_l, c), dev(x, z, y_t, c)

    def remote(src, dst, device, pair_of_sems):
        s, r = pair_of_sems
        return Copy((None, lambda: pltpu.make_async_remote_copy(src_ref=src(), dst_ref=dst(), send_sem=s, recv_sem=r, device_id=device, device_id_type=MESH)))

    def remote_sized(shapes, src, dst, device, pair_of_sems):
        s, r = pair_of_sems

        def make(size):
            return lambda: pltpu.make_async_remote_copy(src_ref=src(*size), dst_ref=dst(*size), send_sem=s, recv_sem=r, device_id=device, device_id_type=MESH)

        return Copy(*((cond, make(size)) for cond, size in shapes))

    def row_big(q):
        return (q < 2) == (c == 0)

    def row_at(q):
        return pl.multiple_of(56 * q + 8 * jnp.where(c == 0, jnp.minimum(q, 2), jnp.maximum(q - 2, 0)), 8)

    def col_big(q):
        return jnp.where(c == 0, q, 3 - q) < 3

    def col_at(q):
        return pl.multiple_of(384 * q + 128 * jnp.where(c == 0, jnp.minimum(q, 3), jnp.maximum(q - 1, 0)), 128)

    def rows_of(q):
        big = row_big(q)
        return [(big, (64,)), (jnp.logical_not(big), (56,))]

    def cols_of(q):
        big = col_big(q)
        return [(big, (512,)), (jnp.logical_not(big), (384,))]

    def cells_of(qx, qz):
        rb, cb = row_big(qx), col_big(qz)
        nr, nc = jnp.logical_not(rb), jnp.logical_not(cb)
        return [(rb & cb, (64, 512)), (rb & nc, (64, 384)), (nr & cb, (56, 512)), (nr & nc, (56, 384))]

    for part in range(2):
        for j in range(2):
            lraw[part, j, ROWS:PAD, :] = jnp.zeros((PAD - ROWS, V), F32)
    for part in range(4):
        for j in range(2):
            traw[part, j, ROWS:PAD, :] = jnp.zeros((PAD - ROWS, V), F32)

    @pl.when(jnp.logical_not(col_big(z)))
    def _():
        lz[:, :, :, :, 384:512] = jnp.zeros((4, 4, 2, 64, 128), F32)
        tx[:, :, :, :, 384:512] = jnp.zeros((4, 4, 2, 64, 128), F32)

    barrier = pltpu.get_barrier_semaphore()
    peers = [at_x(d) for d in (1, 2, 3)] + [at_z(d) for d in (1, 2, 3)] + [at_y(d) for d in (1, 2, 3)] + [other]
    for peer in peers:
        pl.semaphore_signal(barrier, inc=1, device_id=peer, device_id_type=MESH)
    pl.semaphore_wait(barrier, len(peers))

    def cut(i):
        j, k = divmod(i, KPARTS)
        return j, pl.ds(KC * k, KC)

    y_lambda, y_amps, forward = [], [], []
    for i in range(STEPS):
        j, cols = cut(i)
        y_lambda.append(remote(lambda j=j, cols=cols: l_ref.at[j, :, cols], lambda j=j, cols=cols: lraw.at[1, j, pl.ds(0, ROWS), cols], to_l, sems.take()))
        y_amps.append(remote(lambda j=j, cols=cols: t_ref.at[j, :, cols], lambda j=j, cols=cols: traw.at[2 + c, j, pl.ds(0, ROWS), cols], to_t, sems.take()))
        here = lambda j=j, cols=cols: traw.at[2 + c, j, pl.ds(0, ROWS), cols]
        forward.append(remote(here, here, other, sems.take()))
    core_amps = [remote(lambda j=j: t_ref.at[j], lambda j=j: traw.at[c, j, pl.ds(0, ROWS), :], other, sems.take()) for j in range(2)]
    own = []
    for j in range(2):
        own.append(pltpu.make_async_copy(l_ref.at[j], lraw.at[0, j, pl.ds(0, ROWS), :], local.at[2 * j]))
        own.append(pltpu.make_async_copy(t_ref.at[j], traw.at[c, j, pl.ds(0, ROWS), :], local.at[2 * j + 1]))

    hop_l = [
        remote_sized(
            rows_of(ring(x + d)),
            lambda r, d=d: l_ref.at[:, pl.ds(row_at(ring(x + d)), r), :],
            lambda r, d=d: lx.at[d - 1, :, pl.ds(0, r), :],
            at_x(d), sems.take(),
        )
        for d in (1, 2, 3)
    ]
    hop_t = [
        remote_sized(
            cols_of(ring(z + d)),
            lambda n, d=d: t_ref.at[:, :, pl.ds(col_at(ring(z + d)), n)],
            lambda n, d=d: tz.at[d - 1, :, :, pl.ds(0, n)],
            at_z(d), sems.take(),
        )
        for d in (1, 2, 3)
    ]
    got_l = [
        remote_sized(rows_of(x), lambda r, d=d: lx.at[d - 1, :, pl.ds(0, r), :], lambda r, d=d: lx.at[d - 1, :, pl.ds(0, r), :], at_x(d), (send.at[6 * 3 + 2 + d - 1], recv.at[6 * 3 + 2 + d - 1]))
        for d in (1, 2, 3)
    ]
    got_t = [
        remote_sized(cols_of(z), lambda n, d=d: tz.at[d - 1, :, :, pl.ds(0, n)], lambda n, d=d: tz.at[d - 1, :, :, pl.ds(0, n)], at_z(d), (send.at[6 * 3 + 5 + d - 1], recv.at[6 * 3 + 5 + d - 1]))
        for d in (1, 2, 3)
    ]

    second_l, second_t, got2_l, got2_t, keep_l, keep_t = {}, {}, {}, {}, {}, {}
    for d in range(4):

        def from_l(r, n, q, d=d):
            if d == 0:
                return l_ref.at[:, pl.ds(row_at(x), r), pl.ds(col_at(q), n)]
            return lx.at[d - 1, :, pl.ds(0, r), pl.ds(col_at(q), n)]

        def from_t(r, n, q, d=d):
            if d == 0:
                return t_ref.at[:, pl.ds(row_at(q), r), pl.ds(col_at(z), n)]
            return tz.at[d - 1, :, pl.ds(row_at(q), r), pl.ds(0, n)]

        for e in (1, 2, 3):
            s_l, s_t = sems.take(), sems.take()
            second_l[d, e] = remote_sized(
                cells_of(x, ring(z + e)),
                lambda r, n, d=d, e=e, f=from_l: f(r, n, ring(z + e)),
                lambda r, n, d=d: lz.at[ring(x - d), z, :, pl.ds(0, r), pl.ds(0, n)],
                at_z(e), s_l,
            )
            second_t[d, e] = remote_sized(
                cells_of(ring(x + e), z),
                lambda r, n, d=d, e=e, f=from_t: f(r, n, ring(x + e)),
                lambda r, n, d=d: tx.at[x, ring(z - d), :, pl.ds(0, r), pl.ds(0, n)],
                at_x(e), s_t,
            )
            land_l = lambda r, n, d=d, e=e: lz.at[ring(x - d), ring(z - e), :, pl.ds(0, r), pl.ds(0, n)]
            land_t = lambda r, n, d=d, e=e: tx.at[ring(x - e), ring(z - d), :, pl.ds(0, r), pl.ds(0, n)]
            got2_l[d, e] = remote_sized(cells_of(x, z), land_l, land_l, at_z(e), s_l)
            got2_t[d, e] = remote_sized(cells_of(x, z), land_t, land_t, at_x(e), s_t)

        def make_l(r, n, d=d, f=from_l):
            return lambda: pltpu.make_async_copy(f(r, n, z), lz.at[ring(x - d), z, :, pl.ds(0, r), pl.ds(0, n)], local.at[4 + d])

        def make_t(r, n, d=d, f=from_t):
            return lambda: pltpu.make_async_copy(f(r, n, x), tx.at[x, ring(z - d), :, pl.ds(0, r), pl.ds(0, n)], local.at[8 + d])

        keep_l[d] = Copy(*((cond, make_l(*size)) for cond, size in cells_of(x, z)))
        keep_t[d] = Copy(*((cond, make_t(*size)) for cond, size in cells_of(x, z)))

    for copy in own:
        copy.start()
    for i in range(STEPS):
        y_lambda[i].start()
        y_amps[i].start()
        if i == 0:
            for d in (0, 2, 1):
                hop_l[d].start()
                hop_t[d].start()
            core_amps[0].start()
            core_amps[1].start()
    for e in (1, 3, 2):
        second_l[0, e].start()
        second_t[0, e].start()
    keep_l[0].start()
    keep_t[0].start()

    acc[...] = jnp.zeros_like(acc)

    def multiply(i):
        j, cols = cut(i)
        for part in range(2):

            @pl.loop(0, PAD // 32)
            def _(b, part=part):
                at = pl.multiple_of(b * 32, 32)
                hi, lo = split(lraw[part, j, pl.ds(at, 32), cols])
                rows = pl.ds(part * PAD + at, 32)
                lcat[rows, 0:KC] = hi
                lcat[rows, KC : 2 * KC] = lo
                lcat[rows, 2 * KC :] = hi

        for slot in range(8):

            @pl.loop(0, 4)
            def _(b, slot=slot):
                at = pl.multiple_of(b * 32, 32)
                hi, lo = split(traw[slot // 2, j, pl.ds(120 * (slot % 2) + at, 32), cols])
                rows = pl.ds(slot * 128 + at, 32)
                tcat[rows, 0:KC] = hi
                tcat[rows, KC : 2 * KC] = hi
                tcat[rows, 2 * KC :] = lo

        @pl.loop(0, 4)
        def _(n):
            rhs = tcat[pl.ds(pl.multiple_of(n * 256, 256), 256), :]

            @pl.loop(0, 2)
            def _(m):
                rows = pl.ds(pl.multiple_of(m * 256, 256), 256)
                r = dot_nt(lcat[rows, :], rhs)
                acc[n // 2, 2 * (n % 2), rows, :] += r[:, :128]
                acc[n // 2, 2 * (n % 2) + 1, rows, :] += r[:, 128:]

    for copy in own:
        copy.wait()
    for i in range(STEPS):
        y_amps[i].wait_recv()
        forward[i].start()
        y_lambda[i].wait_recv()
        if i % KPARTS == 0:
            core_amps[i // KPARTS].wait_recv()
        forward[i].wait_recv()
        multiply(i)
        if i == 2:
            for d in (1, 3, 2):
                got_l[d - 1].wait_recv()
                for e in (1, 3, 2):
                    second_l[d, e].start()
                keep_l[d].start()
                got_t[d - 1].wait_recv()
                for e in (1, 3, 2):
                    second_t[d, e].start()
                keep_t[d].start()

    part_o, part_p, cells_o, cells_p, last, y_move = {}, {}, {}, {}, {}, None
    for d in (1, 2, 3):
        part_o[d] = remote(lambda d=d: acc.at[:, ring(z + d), pl.ds(0, 256), :], lambda d=d: ro1.at[d - 1], at_z(d), sems.take())
        part_p[d] = remote(lambda d=d: acc.at[:, :, pl.ds(pl.multiple_of(256 + 64 * ring(x + d), 64), 64), :], lambda d=d: rp1.at[d - 1], at_x(d), sems.take())
        cells_o[d] = remote(lambda d=d: so.at[:, pl.ds(pl.multiple_of(64 * ring(x + d), 64), 64), :], lambda d=d: ro2.at[d - 1], at_x(d), sems.take())
        cells_p[d] = remote(lambda d=d: sp.at[:, ring(z + d)], lambda d=d: rp2.at[d - 1], at_z(d), sems.take())
    y_move = remote(lambda: fp, lambda: yq, to_l, sems.take())
    for d in (1, 3, 2):
        part_o[d].start()
        part_p[d].start()

    for d in range(4):
        keep_l[d].wait()
        keep_t[d].wait()
        for e in (1, 2, 3):
            got2_l[d, e].wait_recv()
            got2_t[d, e].wait_recv()
    gram[...] = jnp.zeros_like(gram)

    @pl.loop(0, jnp.where(row_big(x), 8, 7))
    def _(b):
        rows = pl.ds(pl.multiple_of(b * 8, 8), 8)
        a_hi, a_lo = split(lz[:, :, :, rows, :].reshape(256, 512))
        b_hi, b_lo = split(tx[:, :, :, rows, :].reshape(256, 512))
        gram[...] += dot_nt(a_hi, b_hi) + (dot_nt(a_lo, b_hi) + dot_nt(a_hi, b_lo))

    row = lax.broadcasted_iota(jnp.int32, (256, 256), 0)
    col = lax.broadcasted_iota(jnp.int32, (256, 256), 1)
    same = lax.rem(row, 8) == lax.rem(col, 8)
    by_row = jnp.where(same, gram[...], 0.0).reshape(NP, 8, 256).sum(axis=1)
    pick = lax.broadcasted_iota(jnp.int32, (256, 128), 0)
    pick = (lax.div(pick, 8) == lax.broadcasted_iota(jnp.int32, (256, 128), 1)).astype(F32)
    inter = lax.dot_general(by_row, pick, (((1,), (0,)), ((), ())), precision=lax.Precision.HIGHEST, preferred_element_type=F32)

    def share(buf, me, places, value):
        buf[me] = value
        copies = []
        for d, place in places:
            copy = remote(lambda: buf.at[me], lambda: buf.at[me], place, sems.take())
            copy.start()
            copies.append(copy)
        return copies

    def total(buf, copies, n):
        for copy in copies:
            copy.wait_recv()
        value = buf[0]
        for k in range(1, n):
            value = value + buf[k]
        return value

    over_x = share(ix, x, [(d, at_x(d)) for d in (1, 2, 3)], inter)

    for d in (1, 3, 2):
        part_o[d].wait_recv()
    for part in range(2):
        so[part] = (acc[part, z, 0:256, :] + ro1[0, part]) + (ro1[1, part] + ro1[2, part])
    for d in (1, 3, 2):
        cells_o[d].start()
    for d in (1, 3, 2):
        part_p[d].wait_recv()
    mine = pl.ds(pl.multiple_of(256 + 64 * x, 64), 64)
    for part in range(2):
        for q in range(4):
            sp[part, q] = (acc[part, q, mine, :] + rp1[0, part, q]) + (rp1[1, part, q] + rp1[2, part, q])
    for d in (1, 3, 2):
        cells_p[d].start()

    over_z = share(iz, z, [(d, at_z(d)) for d in (1, 2, 3)], total(ix, over_x, 4))

    for d in (1, 3, 2):
        cells_p[d].wait_recv()
    for part in range(2):
        fp[part] = (sp[part, z] + rp2[0, part]) + (rp2[1, part] + rp2[2, part])
    y_move.start()
    for d in (1, 3, 2):
        cells_o[d].wait_recv()
    mine = pl.ds(pl.multiple_of(64 * x, 64), 64)
    for part in range(2):
        fo[part] = (so[part, mine, :] + ro2[0, part]) + (ro2[1, part] + ro2[2, part])

    lasts = []
    for src, b in ((fo, y), (fo, y_t), (yq, y_l), (yq, 3 - y_l)):
        k = len(lasts)
        s = sems.take()
        block = lambda src=src, k=k: src.at[k % 2]
        away, stays = b != x, b == x
        go = Copy((away, lambda block=block, b=b, s=s: pltpu.make_async_remote_copy(src_ref=block(), dst_ref=fin.at[x], send_sem=s[0], recv_sem=recv.at[N_SEMS - 4 + x], device_id=dev(b, z, y, c), device_id_type=MESH)))
        stay = Copy((stays, lambda block=block: pltpu.make_async_copy(block(), fin.at[x], local.at[12])))
        lasts.append((go, stay))
    for go, stay in lasts[:2]:
        go.start()
        stay.start()
    over_y = share(iy, y, [(d, at_y(d)) for d in (1, 2, 3)], total(iz, over_z, 4))
    y_move.wait_recv()
    for go, stay in lasts[2:]:
        go.start()
        stay.start()
    over_c = share(ic, c, [(1, other)], total(iy, over_y, 4))
    for go, stay in lasts:
        stay.wait()
    for d in (1, 2, 3):
        q = ring(x - d)
        pltpu.make_async_remote_copy(src_ref=fin.at[q], dst_ref=fin.at[q], send_sem=send.at[0], recv_sem=recv.at[N_SEMS - 4 + q], device_id=at_x(d), device_id_type=MESH).wait_recv()
    out_ref[...] = fin[...].reshape(256, 128)[:ROWS, :120]
    inter_ref[...] = total(ic, over_c, 2)

    sent = y_lambda + y_amps + forward + core_amps + hop_l + hop_t + list(second_l.values()) + list(second_t.values())
    sent += [y_move] + [go for go, _ in lasts] + over_x + over_z + over_y + over_c
    for group in (part_o, part_p, cells_o, cells_p):
        sent += list(group.values())
    for copy in sent:
        copy.wait_send()


def shards(lambda_blocks, amplitudes, pair_list):
    highest = lax.Precision.HIGHEST
    vmem = lambda shape, dtype=F32: pltpu.VMEM(shape, dtype)
    density_virt, intersection = pl.pallas_call(
        kernel,
        out_shape=(jax.ShapeDtypeStruct((ROWS, 120), F32), jax.ShapeDtypeStruct((NP, 128), F32)),
        in_specs=[pl.BlockSpec(memory_space=pl.ANY)] * 2,
        out_specs=(pl.BlockSpec(memory_space=pltpu.VMEM),) * 2,
        scratch_shapes=[
            vmem((2, 2, PAD, V)), vmem((4, 2, PAD, V)), vmem((512, 3 * KC), BF16), vmem((1024, 3 * KC), BF16), vmem((2, 4, 512, 128)),
            vmem((3, 2, 64, V)), vmem((3, 2, ROWS, 512)), vmem((4, 4, 2, 64, 512)), vmem((4, 4, 2, 64, 512)), vmem((256, 256)),
            vmem((3, 2, 256, 128)), vmem((3, 2, 64, 128)), vmem((3, 2, 4, 64, 128)), vmem((3, 2, 64, 128)),
            vmem((2, 256, 128)), vmem((2, 4, 64, 128)), vmem((2, 64, 128)), vmem((2, 64, 128)), vmem((2, 64, 128)), vmem((4, 64, 128)),
            vmem((4, NP, 128)), vmem((4, NP, 128)), vmem((4, NP, 128)), vmem((2, NP, 128)),
            pltpu.SemaphoreType.DMA((N_SEMS,)), pltpu.SemaphoreType.DMA((N_SEMS,)), pltpu.SemaphoreType.DMA((13,)),
        ],
        compiler_params=pltpu.CompilerParams(collective_id=0, has_side_effects=True, vmem_limit_bytes=60 * 2**20),
        cost_estimate=pl.CostEstimate(flops=12_000_000_000, bytes_accessed=8_000_000, transcendentals=0),
    )(lambda_blocks, amplitudes)
    intersection = intersection[:, :NP]
    first = pair_list[:, 0]
    second = pair_list[:, 1]
    one_hot = (first[:, None] == jnp.arange(OCC, dtype=jnp.int32)[None, :]).astype(F32)
    same_k = (second[:, None] == second[None, :]).astype(F32)
    inner = jnp.dot(same_k * intersection, one_hot, precision=highest)
    density_occ = -jnp.dot(one_hot.T, inner, precision=highest)
    return (density_virt, density_occ)


def solution(mesh):
    in_specs = (P("pair", "virt", None), P("pair", "virt", None), P())
    out_specs = (P("virt", "pair"), P())
    return jax.shard_map(shards, mesh=mesh, in_specs=in_specs, out_specs=out_specs, check_vma=False)
```

```python
import jax
import jax.numpy as jnp
from jax import lax
from jax.experimental import pallas as pl
from jax.experimental.pallas import tpu as pltpu
from jax.sharding import PartitionSpec as P

OCC = 200
NP = 32
ROWS = 240
PAD = 256
V = 1920
CUTS = ((0, 0, 640), (0, 640, 640), (0, 1280, 640), (1, 0, 640), (1, 640, 640), (1, 1280, 384), (1, 1664, 256))
OWN_CUTS = ((0, 0, 640), (0, 640, 640), (0, 1280, 640), (1, 0, 640), (1, 640, 640), (1, 1280, 640))
KC = 640
STEPS = len(CUTS)
MESH = pl.DeviceIdType.MESH
F32 = jnp.float32
BF16 = jnp.bfloat16


class Copy:
    def __init__(self, *variants):
        self.variants = variants

    def _each(self, act):
        for cond, make in self.variants:
            if cond is None:
                act(make())
            else:

                @pl.when(cond)
                def _(make=make):
                    act(make())

    def start(self):
        self._each(lambda c: c.start())

    def wait_send(self):
        self._each(lambda c: c.wait_send())

    def wait_recv(self):
        self._each(lambda c: c.wait_recv())

    def wait(self):
        self._each(lambda c: c.wait())


class Sems:
    def __init__(self, send, recv):
        self.send, self.recv, self.n = send, recv, 0

    def take(self):
        self.n += 1
        return self.send.at[self.n - 1], self.recv.at[self.n - 1]


def split(v):
    hi = v.astype(BF16)
    return hi, (v - hi.astype(F32)).astype(BF16)


NT = (((1,), (1,)), ((), ()))


def dot_nt(a, b):
    return lax.dot_general(a, b, NT, preferred_element_type=F32)


N_SEMS = 160


def kernel(
    l_ref, t_ref, pair_ref, fin, occ_ref,
    lraw, traw, lcat, tcat, acc, lx, tz, lz, tx, gram,
    rz1, rx1, rz2, rx2, sz, sx, done, ig, ip, pair_list,
    send, recv, local,
):
    pair, virt = lax.axis_index("pair"), lax.axis_index("virt")
    x, z = lax.div(pair, 4), lax.rem(pair, 4)
    y, c = lax.div(virt, 2), lax.rem(virt, 2)
    sems = Sems(send, recv)

    def ring(a):
        return lax.rem(a + 4, 4)

    def dev(xx, zz, yy, cc):
        return (xx * 4 + zz, yy * 2 + cc)

    def at_x(d):
        return dev(ring(x + d), z, y, c)

    def at_z(d):
        return dev(x, ring(z + d), y, c)

    def at_y(d):
        return dev(x, z, ring(y + d), c)

    other = dev(x, z, y, 1 - c)
    y_l = y + 1 - 2 * lax.rem(y, 2)
    y_t = 3 - y
    to_l, to_t = dev(x, z, y_l, c), dev(x, z, y_t, c)

    def remote(src, dst, device, pair_of_sems):
        s, r = pair_of_sems
        return Copy((None, lambda: pltpu.make_async_remote_copy(src_ref=src(), dst_ref=dst(), send_sem=s, recv_sem=r, device_id=device, device_id_type=MESH)))

    def remote_sized(shapes, src, dst, device, pair_of_sems):
        s, r = pair_of_sems

        def make(size):
            return lambda: pltpu.make_async_remote_copy(src_ref=src(*size), dst_ref=dst(*size), send_sem=s, recv_sem=r, device_id=device, device_id_type=MESH)

        return Copy(*((cond, make(size)) for cond, size in shapes))

    def row_big(q):
        return (q < 2) == (c == 0)

    def row_at(q):
        return pl.multiple_of(56 * q + 8 * jnp.where(c == 0, jnp.minimum(q, 2), jnp.maximum(q - 2, 0)), 8)

    def col_big(q):
        return lax.div(q, 2) != c

    def col_at(q):
        return pl.multiple_of(512 * q - 128 * jnp.where((c == 0) & (q > 1), 1, 0), 128)

    shared = pl.ds(pl.multiple_of(384 + 1024 * c, 128), 128)
    aside = pl.ds(384, 128)

    def shared_at(q):
        return 32 * (1 - lax.rem(q, 2))

    def shared_of(qx, qz):
        short, odd, big = jnp.logical_not(col_big(qz)), lax.rem(qz, 2) == 1, row_big(qx)
        narrow = jnp.logical_not(odd) & jnp.logical_not(big)
        return [(short & jnp.logical_not(narrow), (32,)), (short & narrow, (24,))]

    def some(at, r):
        return pl.ds(pl.multiple_of(at, 8), r)

    def rows_of(q):
        big = row_big(q)
        return [(big, (64,)), (jnp.logical_not(big), (56,))]

    def cols_of(q):
        big = col_big(q)
        return [(big, (512,)), (jnp.logical_not(big), (384,))]

    def cells_of(qx, qz):
        rb, cb = row_big(qx), col_big(qz)
        nr, nc = jnp.logical_not(rb), jnp.logical_not(cb)
        return [(rb & cb, (64, 512)), (rb & nc, (64, 384)), (nr & cb, (56, 512)), (nr & nc, (56, 384))]

    barrier = pltpu.get_barrier_semaphore()
    around = [(dy, dc) for dy in range(4) for dc in range(2) if (dy, dc) != (0, 0)]
    plane = [(dx, dz) for dx in range(4) for dz in range(4) if (dx, dz) != (0, 0)]
    at_group = [dev(x, z, ring(y + dy), lax.rem(c + dc, 2)) for dy, dc in around]
    at_plane = [dev(ring(x + dx), ring(z + dz), y, c) for dx, dz in plane]
    peers = at_group + at_plane + [dev(ring(x + d), z, y_l, c) for d in (1, 2, 3)]
    for peer in peers:
        pl.semaphore_signal(barrier, inc=1, device_id=peer, device_id_type=MESH)
    pl.semaphore_wait(barrier, len(peers))

    def cut(i):
        j, first, n = CUTS[i]
        return j, pl.ds(first, n)

    y_lambda, y_amps, forward = [], [], []
    for i in range(STEPS):
        j, cols = cut(i)
        y_lambda.append(remote(lambda j=j, cols=cols: l_ref.at[j, :, cols], lambda j=j, cols=cols: lraw.at[1, j, pl.ds(0, ROWS), cols], to_l, sems.take()))
        y_amps.append(remote(lambda j=j, cols=cols: t_ref.at[j, :, cols], lambda j=j, cols=cols: traw.at[2 + c, j, pl.ds(0, ROWS), cols], to_t, sems.take()))
        here = lambda j=j, cols=cols: traw.at[2 + c, j, pl.ds(0, ROWS), cols]
        forward.append(remote(here, here, other, sems.take()))
    core_amps = [remote(lambda j=j: t_ref.at[j], lambda j=j: traw.at[c, j, pl.ds(0, ROWS), :], other, sems.take()) for j in range(2)]
    own = []
    for j in range(2):
        own.append(pltpu.make_async_copy(l_ref.at[j], lraw.at[0, j, pl.ds(0, ROWS), :], local.at[2 * j]))
        own.append(pltpu.make_async_copy(t_ref.at[j], traw.at[c, j, pl.ds(0, ROWS), :], local.at[2 * j + 1]))

    hop_l = [
        remote_sized(
            rows_of(ring(x + d)),
            lambda r, d=d: l_ref.at[:, pl.ds(row_at(ring(x + d)), r), :],
            lambda r, d=d: lx.at[d - 1, :, pl.ds(0, r), :],
            at_x(d), sems.take(),
        )
        for d in (1, 2, 3)
    ]
    hop_t = [
        remote_sized(
            cols_of(ring(z + d)),
            lambda n, d=d: t_ref.at[:, :, pl.ds(col_at(ring(z + d)), n)],
            lambda n, d=d: tz.at[d - 1, :, :, pl.ds(0, n)],
            at_z(d), sems.take(),
        )
        for d in (1, 2, 3)
    ]
    hop_s, got_s = {}, {}
    for d in (1, 2, 3):
        for q in range(4):
            s_q = sems.take()
            to = ring(z + d)
            hop_s[d, q] = remote_sized(
                shared_of(q, to),
                lambda r, q=q, to=to: t_ref.at[:, some(row_at(q) + shared_at(to), r), shared],
                lambda r, d=d, q=q, to=to: tz.at[d - 1, :, some(row_at(q) + shared_at(to), r), aside],
                at_z(d), s_q,
            )
            land = lambda r, d=d, q=q: tz.at[d - 1, :, some(row_at(q) + shared_at(z), r), aside]
            got_s[d, q] = remote_sized(shared_of(q, z), land, land, at_z(d), s_q)
    got_l = [
        remote_sized(rows_of(x), lambda r, d=d: lx.at[d - 1, :, pl.ds(0, r), :], lambda r, d=d: lx.at[d - 1, :, pl.ds(0, r), :], at_x(d), (send.at[3 * STEPS + 2 + d - 1], recv.at[3 * STEPS + 2 + d - 1]))
        for d in (1, 2, 3)
    ]
    got_t = [
        remote_sized(cols_of(z), lambda n, d=d: tz.at[d - 1, :, :, pl.ds(0, n)], lambda n, d=d: tz.at[d - 1, :, :, pl.ds(0, n)], at_z(d), (send.at[3 * STEPS + 5 + d - 1], recv.at[3 * STEPS + 5 + d - 1]))
        for d in (1, 2, 3)
    ]

    more_l, more_t, got_more_l, got_more_t, hold = {}, {}, {}, {}, {}
    second_l, second_t, got2_l, got2_t, keep_l, keep_t = {}, {}, {}, {}, {}, {}
    for d in range(4):

        def from_l(r, n, q, d=d):
            if d == 0:
                return l_ref.at[:, pl.ds(row_at(x), r), pl.ds(col_at(q), n)]
            return lx.at[d - 1, :, pl.ds(0, r), pl.ds(col_at(q), n)]

        def from_t(r, n, q, d=d):
            if d == 0:
                return t_ref.at[:, pl.ds(row_at(q), r), pl.ds(col_at(z), n)]
            return tz.at[d - 1, :, pl.ds(row_at(q), r), pl.ds(0, n)]

        def shared_l(r, q, d=d):
            if d == 0:
                return l_ref.at[:, some(row_at(x) + shared_at(q), r), shared]
            return lx.at[d - 1, :, some(shared_at(q), r), shared]

        def shared_t(r, q, d=d):
            if d == 0:
                return t_ref.at[:, some(row_at(q) + shared_at(z), r), shared]
            return tz.at[d - 1, :, some(row_at(q) + shared_at(z), r), aside]

        for e in (1, 2, 3):
            s_l, s_t = sems.take(), sems.take()
            qx, qz = ring(x + e), ring(z + e)
            more_l[d, e] = remote_sized(
                shared_of(x, qz),
                lambda r, qz=qz, f=shared_l: f(r, qz),
                lambda r, d=d, qz=qz: lz.at[ring(x - d), z, :, some(shared_at(qz), r), aside],
                at_z(e), s_l,
            )
            more_t[d, e] = remote_sized(
                shared_of(qx, z),
                lambda r, qx=qx, f=shared_t: f(r, qx),
                lambda r, d=d: tx.at[x, ring(z - d), :, some(shared_at(z), r), aside],
                at_x(e), s_t,
            )
            land_l = lambda r, d=d, e=e: lz.at[ring(x - d), ring(z - e), :, some(shared_at(z), r), aside]
            land_t = lambda r, d=d, e=e: tx.at[ring(x - e), ring(z - d), :, some(shared_at(z), r), aside]
            got_more_l[d, e] = remote_sized(shared_of(x, z), land_l, land_l, at_z(e), s_l)
            got_more_t[d, e] = remote_sized(shared_of(x, z), land_t, land_t, at_x(e), s_t)

        def hold_l(r, d=d, f=shared_l):
            return lambda: pltpu.make_async_copy(f(r, z), lz.at[ring(x - d), z, :, some(shared_at(z), r), aside], local.at[14 + d])

        def hold_t(r, d=d, f=shared_t):
            return lambda: pltpu.make_async_copy(f(r, x), tx.at[x, ring(z - d), :, some(shared_at(z), r), aside], local.at[18 + d])

        hold[d] = [Copy(*((cond, h(*size)) for cond, size in shared_of(x, z))) for h in (hold_l, hold_t)]

        for e in (1, 2, 3):
            s_l, s_t = sems.take(), sems.take()
            second_l[d, e] = remote_sized(
                cells_of(x, ring(z + e)),
                lambda r, n, d=d, e=e, f=from_l: f(r, n, ring(z + e)),
                lambda r, n, d=d: lz.at[ring(x - d), z, :, pl.ds(0, r), pl.ds(0, n)],
                at_z(e), s_l,
            )
            second_t[d, e] = remote_sized(
                cells_of(ring(x + e), z),
                lambda r, n, d=d, e=e, f=from_t: f(r, n, ring(x + e)),
                lambda r, n, d=d: tx.at[x, ring(z - d), :, pl.ds(0, r), pl.ds(0, n)],
                at_x(e), s_t,
            )
            land_l = lambda r, n, d=d, e=e: lz.at[ring(x - d), ring(z - e), :, pl.ds(0, r), pl.ds(0, n)]
            land_t = lambda r, n, d=d, e=e: tx.at[ring(x - e), ring(z - d), :, pl.ds(0, r), pl.ds(0, n)]
            got2_l[d, e] = remote_sized(cells_of(x, z), land_l, land_l, at_z(e), s_l)
            got2_t[d, e] = remote_sized(cells_of(x, z), land_t, land_t, at_x(e), s_t)

        def make_l(r, n, d=d, f=from_l):
            return lambda: pltpu.make_async_copy(f(r, n, z), lz.at[ring(x - d), z, :, pl.ds(0, r), pl.ds(0, n)], local.at[4 + d])

        def make_t(r, n, d=d, f=from_t):
            return lambda: pltpu.make_async_copy(f(r, n, x), tx.at[x, ring(z - d), :, pl.ds(0, r), pl.ds(0, n)], local.at[8 + d])

        keep_l[d] = Copy(*((cond, make_l(*size)) for cond, size in cells_of(x, z)))
        keep_t[d] = Copy(*((cond, make_t(*size)) for cond, size in cells_of(x, z)))

    pairs = pltpu.make_async_copy(pair_ref, pair_list, local.at[13])
    pairs.start()
    for copy in own:
        copy.start()
    for i in range(STEPS):
        y_lambda[i].start()
        y_amps[i].start()
        if i == 0:
            for d in (0, 2, 1):
                hop_l[d].start()
                hop_t[d].start()
                for q in range(4):
                    hop_s[d + 1, q].start()
            core_amps[0].start()
            core_amps[1].start()
    for e in (1, 3, 2):
        second_l[0, e].start()
        more_l[0, e].start()
        second_t[0, e].start()
        more_t[0, e].start()
    for copy in (keep_l[0], keep_t[0], *hold[0]):
        copy.start()

    for part in range(2):
        for j in range(2):
            lraw[part, j, ROWS:PAD, :] = jnp.zeros((PAD - ROWS, V), F32)
    for part in range(4):
        for j in range(2):
            traw[part, j, ROWS:PAD, :] = jnp.zeros((PAD - ROWS, V), F32)

    @pl.when(jnp.logical_not(col_big(z)))
    def _():
        empty = pl.ds(pl.multiple_of(32 - shared_at(z), 32), 32)
        lz[:, :, :, empty, aside] = jnp.zeros((4, 4, 2, 32, 128), F32)
        tx[:, :, :, empty, aside] = jnp.zeros((4, 4, 2, 32, 128), F32)

    acc[...] = jnp.zeros_like(acc)
    gram[...] = jnp.zeros_like(gram)

    def halves(j, first, n, blocks, parts_l, parts_t):
        cols = pl.ds(first, n)
        for part in parts_l:

            @pl.loop(0, PAD // 32)
            def _(b, part=part):
                at = pl.multiple_of(b * 32, 32)
                hi, lo = split(lraw[part, j, pl.ds(at, 32), cols])
                rows = pl.ds(part * PAD + at, 32)
                lcat[rows, 0:n] = hi
                lcat[rows, n : 2 * n] = lo
                lcat[rows, 2 * n : 3 * n] = hi

        for slot in parts_t:

            @pl.loop(0, 4)
            def _(b, slot=slot):
                at = pl.multiple_of(b * 32, 32)
                hi, lo = split(traw[slot // 2, j, pl.ds(120 * (slot % 2) + at, 32), cols])
                rows = pl.ds(slot * 128 + at, 32)
                tcat[rows, 0:n] = hi
                tcat[rows, n : 2 * n] = hi
                tcat[rows, 2 * n : 3 * n] = lo

        for n_range, m in blocks:

            @pl.loop(*n_range)
            def _(b, m=m):
                r = dot_nt(lcat[m * 256 : (m + 1) * 256, 0 : 3 * n], tcat[pl.ds(pl.multiple_of(b * 256, 256), 256), 0 : 3 * n])
                rows = slice(m * 256, (m + 1) * 256)
                acc[b // 2, 2 * (b % 2), rows, :] += r[:, :128]
                acc[b // 2, 2 * (b % 2) + 1, rows, :] += r[:, 128:]

    def lo(h):
        return pl.ds(256 * h, 128)

    def hi_of(h, q):
        return pl.ds(pl.multiple_of(256 * h + 128 + 32 * q, 32), 32)

    early, late, second = [], ([], []), ({}, {})
    for d in (1, 3, 2):
        qx, qz = ring(x + d), ring(z + d)
        early.append(remote(lambda qz=qz: acc.at[0, qz, lo(0), :], lambda d=d: rz1.at[d - 1, 0, 0], at_z(d), sems.take()))
        early.append(remote(lambda qx=qx: acc.at[0, :, hi_of(0, qx), :], lambda d=d: rx1.at[d - 1, 0, 0], at_x(d), sems.take()))
        late[0].append(remote(lambda qz=qz: acc.at[1, qz, lo(0), :], lambda d=d: rz1.at[d - 1, 0, 1], at_z(d), sems.take()))
        late[0].append(remote(lambda qx=qx: acc.at[1, :, hi_of(0, qx), :], lambda d=d: rx1.at[d - 1, 0, 1], at_x(d), sems.take()))
        late[1].append(remote(lambda qz=qz: acc.at[:, qz, lo(1), :], lambda d=d: rz1.at[d - 1, 1], at_z(d), sems.take()))
        late[1].append(remote(lambda qx=qx: acc.at[:, :, hi_of(1, qx), :], lambda d=d: rx1.at[d - 1, 1], at_x(d), sems.take()))
        for h in range(2):
            second[h]["z", d] = remote(lambda qx=qx, h=h: sz.at[h, :, pl.ds(pl.multiple_of(32 * qx, 32), 32), :], lambda d=d, h=h: rz2.at[d - 1, h], at_x(d), sems.take())
            second[h]["x", d] = remote(lambda qz=qz, h=h: sx.at[h, :, qz], lambda d=d, h=h: rx2.at[d - 1, h], at_z(d), sems.take())

    for copy in own:
        copy.wait()
    for k, (j, first, n) in enumerate(OWN_CUTS):
        if k % 3 == 0:
            core_amps[j].wait_recv()
        halves(j, first, n, [((0, 2), 0)], (0,), range(4))
    for copy in early:
        copy.start()
    for i in range(STEPS):
        y_amps[i].wait_recv()
        forward[i].start()
        y_lambda[i].wait_recv()
        forward[i].wait_recv()
        halves(*CUTS[i], [((0, 4), 1), ((2, 4), 0)], (0, 1), range(8))
        if i == 2:
            for d in (1, 3, 2):
                got_l[d - 1].wait_recv()
                for e in (1, 3, 2):
                    second_l[d, e].start()
                    more_l[d, e].start()
                keep_l[d].start()
                got_t[d - 1].wait_recv()
                for q in range(4):
                    got_s[d, q].wait_recv()
                for e in (1, 3, 2):
                    second_t[d, e].start()
                    more_t[d, e].start()
                keep_t[d].start()
                for copy in hold[d]:
                    copy.start()
    for copy in late[0] + late[1]:
        copy.start()

    for d in range(4):
        keep_l[d].wait()
        keep_t[d].wait()
        for copy in hold[d]:
            copy.wait()
        for e in (1, 2, 3):
            for came in (got2_l, got2_t, got_more_l, got_more_t):
                came[d, e].wait_recv()
    @pl.loop(0, jnp.where(row_big(x), 8, 7))
    def _(b):
        rows = pl.ds(pl.multiple_of(b * 8, 8), 8)
        a_hi, a_lo = split(lz[:, :, :, rows, :].reshape(256, 512))
        b_hi, b_lo = split(tx[:, :, :, rows, :].reshape(256, 512))
        gram[...] += dot_nt(a_hi, b_hi) + (dot_nt(a_lo, b_hi) + dot_nt(a_hi, b_lo))

    row = lax.broadcasted_iota(jnp.int32, (256, 256), 0)
    col = lax.broadcasted_iota(jnp.int32, (256, 256), 1)
    same = lax.rem(row, 8) == lax.rem(col, 8)
    by_row = jnp.where(same, gram[...], 0.0).reshape(NP, 8, 256).sum(axis=1)
    pick = lax.broadcasted_iota(jnp.int32, (256, 128), 0)
    lane = lax.broadcasted_iota(jnp.int32, (256, 128), 1)
    inter = jnp.zeros((8, 128), F32)
    for k in range(4):
        wanted = (lax.div(pick, 8) + 32 * k == lane).astype(F32)
        inter += lax.dot_general(by_row[8 * k : 8 * k + 8], wanted, (((1,), (0,)), ((), ())), precision=lax.Precision.HIGHEST, preferred_element_type=F32)

    def share(buf, me, places, value):
        buf[me] = value
        copies = [remote(lambda: buf.at[me], lambda: buf.at[me], place, sems.take()) for place in places]
        for copy in copies:
            copy.start()
        return copies

    def total(buf, copies, n):
        for copy in copies:
            copy.wait_recv()
        value = buf[0]
        for k in range(1, n):
            value = value + buf[k]
        return value

    over_group = share(ig, virt, at_group, inter)

    def sum_first(h):
        for copy in (early if h == 0 else []) + late[h]:
            copy.wait_recv()
        for b in range(2):
            sz[h, b] = (acc[b, z, lo(h), :] + rz1[0, h, b]) + (rz1[1, h, b] + rz1[2, h, b])
        for d in (1, 3, 2):
            second[h]["z", d].start()
        for b in range(2):
            for q in range(4):
                sx[h, b, q] = (acc[b, q, hi_of(h, x), :] + rx1[0, h, b, q]) + (rx1[1, h, b, q] + rx1[2, h, b, q])
        for d in (1, 3, 2):
            second[h]["x", d].start()

    lasts = []

    def sum_second(h):
        for copy in second[h].values():
            copy.wait_recv()
        mine = pl.ds(pl.multiple_of(32 * x, 32), 32)
        for b, q in ((0, y), (1, y_t)):
            done[h, b, 0] = (sz[h, b, mine, :] + rz2[0, h, b]) + (rz2[1, h, b] + rz2[2, h, b])
            done[h, b, 1] = (sx[h, b, z] + rx2[0, h, b]) + (rx2[1, h, b] + rx2[2, h, b])
            s = sems.take()[0]
            make = lambda b=b, q=q, s=s: pltpu.make_async_remote_copy(src_ref=done.at[h, b], dst_ref=fin.at[:, x], send_sem=s, recv_sem=recv.at[N_SEMS - 4 + x], device_id=dev(q, z, (y, y_l)[h], c), device_id_type=MESH)
            if h == 0:
                go = Copy((q != x, make))
                stay = Copy((q == x, lambda b=b: pltpu.make_async_copy(done.at[0, b], fin.at[:, x], local.at[12])))
                stay.start()
            else:
                go, stay = Copy((None, make)), Copy()
            go.start()
            lasts.append((go, stay))

    sum_first(0)
    over_plane = share(ip, pair, at_plane, total(ig, over_group, 8))
    sum_first(1)
    sum_second(0)
    sum_second(1)

    every = total(ip, over_plane, 16)
    matrix = jnp.concatenate([every[:, 32 * k : 32 * k + 32] for k in range(4)], axis=0)
    pairs.wait()
    first, kind = pair_list[0:1, :], pair_list[1:2, :]
    one_hot = (first == lax.broadcasted_iota(jnp.int32, (256, NP), 0)).astype(F32)
    kind = (kind == lax.broadcasted_iota(jnp.int32, (NP, NP), 0)).astype(F32)
    same_k = lax.dot_general(kind, kind, (((0,), (0,)), ((), ())), preferred_element_type=F32)
    highest = lax.Precision.HIGHEST
    outer = lax.dot_general(one_hot, same_k * matrix, (((1,), (0,)), ((), ())), precision=highest, preferred_element_type=F32)
    occ_ref[...] = -lax.dot_general(outer, one_hot, NT, precision=highest, preferred_element_type=F32)

    for go, stay in lasts:
        stay.wait()
    in_plane = (x == y) | (x == y_t)
    for q in range(4):
        came = Copy((jnp.logical_not(in_plane & (x == q)), lambda q=q: pltpu.make_async_remote_copy(src_ref=done.at[0, 0], dst_ref=fin.at[:, q], send_sem=send.at[0], recv_sem=recv.at[N_SEMS - 4 + q], device_id=to_l, device_id_type=MESH)))
        came.wait_recv()

    sent = y_lambda + y_amps + forward + core_amps + hop_l + hop_t + list(second_l.values()) + list(second_t.values())
    for group in (hop_s, more_l, more_t):
        sent += list(group.values())
    sent += early + late[0] + late[1] + list(second[0].values()) + list(second[1].values()) + [go for go, _ in lasts] + over_group + over_plane
    for copy in sent:
        copy.wait_send()


def finish(fin_ref, occ_in, virt_ref, occ_ref):
    virt_ref[...] = fin_ref[...].reshape(256, 128)[:ROWS, :120]
    occ_ref[...] = occ_in[:OCC, :OCC]


def shards(lambda_blocks, amplitudes, pair_list):
    vmem = lambda shape, dtype=F32: pltpu.VMEM(shape, dtype)
    fin, occ = pl.pallas_call(
        kernel,
        out_shape=(jax.ShapeDtypeStruct((2, 4, 32, 128), F32), jax.ShapeDtypeStruct((256, 256), F32)),
        in_specs=[pl.BlockSpec(memory_space=pl.ANY)] * 3,
        out_specs=(pl.BlockSpec(memory_space=pltpu.VMEM),) * 2,
        scratch_shapes=[
            vmem((2, 2, PAD, V)), vmem((4, 2, PAD, V)), vmem((512, 3 * KC), BF16), vmem((1024, 3 * KC), BF16), vmem((2, 4, 512, 128)),
            vmem((3, 2, 64, V)), vmem((3, 2, ROWS, 512)), vmem((4, 4, 2, 64, 512)), vmem((4, 4, 2, 64, 512)), vmem((256, 256)),
            vmem((3, 2, 2, 128, 128)), vmem((3, 2, 2, 4, 32, 128)), vmem((3, 2, 2, 32, 128)), vmem((3, 2, 2, 32, 128)),
            vmem((2, 2, 128, 128)), vmem((2, 2, 4, 32, 128)), vmem((2, 2, 2, 32, 128)), vmem((8, 8, 128)), vmem((16, 8, 128)), vmem((2, NP), jnp.int32),
            pltpu.SemaphoreType.DMA((N_SEMS,)), pltpu.SemaphoreType.DMA((N_SEMS,)), pltpu.SemaphoreType.DMA((22,)),
        ],
        compiler_params=pltpu.CompilerParams(collective_id=0, has_side_effects=True, vmem_limit_bytes=60 * 2**20),
        cost_estimate=pl.CostEstimate(flops=12_000_000_000, bytes_accessed=8_000_000, transcendentals=0),
    )(lambda_blocks, amplitudes, pair_list.T)
    return pl.pallas_call(
        finish,
        out_shape=(jax.ShapeDtypeStruct((ROWS, 120), F32), jax.ShapeDtypeStruct((OCC, OCC), F32)),
        in_specs=[pl.BlockSpec(memory_space=pltpu.VMEM)] * 2,
        out_specs=(pl.BlockSpec(memory_space=pltpu.VMEM),) * 2,
    )(fin, occ)


def solution(mesh):
    in_specs = (P("pair", "virt", None), P("pair", "virt", None), P())
    out_specs = (P("virt", "pair"), P())
    return jax.shard_map(shards, mesh=mesh, in_specs=in_specs, out_specs=out_specs, check_vma=False)
```

```python
import jax
import jax.numpy as jnp
from jax import lax
from jax.experimental import pallas as pl
from jax.experimental.pallas import tpu as pltpu
from jax.sharding import PartitionSpec as P

OCC = 200
NP = 32
ROWS = 240
PAD = 256
V = 1920
WIDE = ((0, 0, 640), (0, 640, 640), (0, 1280, 640), (1, 0, 640), (1, 640, 640), (1, 1280, 640))
NARROW = WIDE[:5] + ((1, 1280, 384), (1, 1664, 256))
CUTS = tuple((0, cut) for cut in WIDE) + tuple((1, cut) for cut in NARROW)
KC = 640
STEPS = len(CUTS)
MESH = pl.DeviceIdType.MESH
F32 = jnp.float32
BF16 = jnp.bfloat16


class Copy:
    def __init__(self, *variants):
        self.variants = variants

    def _each(self, act):
        for cond, make in self.variants:
            if cond is None:
                act(make())
            else:

                @pl.when(cond)
                def _(make=make):
                    act(make())

    def start(self):
        self._each(lambda c: c.start())

    def wait_send(self):
        self._each(lambda c: c.wait_send())

    def wait_recv(self):
        self._each(lambda c: c.wait_recv())

    def wait(self):
        self._each(lambda c: c.wait())


class Sems:
    def __init__(self, send, recv):
        self.send, self.recv, self.n = send, recv, 0

    def take(self):
        self.n += 1
        return self.send.at[self.n - 1], self.recv.at[self.n - 1]


def split(v):
    hi = v.astype(BF16)
    return hi, (v - hi.astype(F32)).astype(BF16)


NT = (((1,), (1,)), ((), ()))


def dot_nt(a, b):
    return lax.dot_general(a, b, NT, preferred_element_type=F32)


N_SEMS = 192


def kernel(
    l_ref, t_ref, t_halves, pair_ref, fin, occ_ref,
    lraw, traw, lcat, tcat, acc, lx, tz, lz, tx, gram,
    rz1, rx1, rz2, rx2, sz, sx, done, ig, ip, pair_list,
    send, recv, local,
):
    pair, virt = lax.axis_index("pair"), lax.axis_index("virt")
    x, z = lax.div(pair, 4), lax.rem(pair, 4)
    y, c = lax.div(virt, 2), lax.rem(virt, 2)
    sems = Sems(send, recv)

    def ring(a):
        return lax.rem(a + 4, 4)

    def dev(xx, zz, yy, cc):
        return (xx * 4 + zz, yy * 2 + cc)

    def at_x(d):
        return dev(ring(x + d), z, y, c)

    def at_z(d):
        return dev(x, ring(z + d), y, c)

    def at_y(d):
        return dev(x, z, ring(y + d), c)

    other = dev(x, z, y, 1 - c)
    y_l = y + 1 - 2 * lax.rem(y, 2)
    y_t = 3 - y
    to_l, to_t = dev(x, z, y_l, c), dev(x, z, y_t, c)

    def remote(src, dst, device, pair_of_sems):
        s, r = pair_of_sems
        return Copy((None, lambda: pltpu.make_async_remote_copy(src_ref=src(), dst_ref=dst(), send_sem=s, recv_sem=r, device_id=device, device_id_type=MESH)))

    def remote_sized(shapes, src, dst, device, pair_of_sems):
        s, r = pair_of_sems

        def make(size):
            return lambda: pltpu.make_async_remote_copy(src_ref=src(*size), dst_ref=dst(*size), send_sem=s, recv_sem=r, device_id=device, device_id_type=MESH)

        return Copy(*((cond, make(size)) for cond, size in shapes))

    def row_big(q):
        return (q < 2) == (c == 0)

    def row_at(q):
        return pl.multiple_of(56 * q + 8 * jnp.where(c == 0, jnp.minimum(q, 2), jnp.maximum(q - 2, 0)), 8)

    def col_big(q):
        return lax.div(q, 2) != c

    def col_at(q):
        return pl.multiple_of(512 * q - 128 * jnp.where((c == 0) & (q > 1), 1, 0), 128)

    shared = pl.ds(pl.multiple_of(384 + 1024 * c, 128), 128)
    aside = pl.ds(384, 128)

    def shared_at(q):
        return 32 * (1 - lax.rem(q, 2))

    def shared_of(qx, qz):
        short, odd, big = jnp.logical_not(col_big(qz)), lax.rem(qz, 2) == 1, row_big(qx)
        narrow = jnp.logical_not(odd) & jnp.logical_not(big)
        return [(short & jnp.logical_not(narrow), (32,)), (short & narrow, (24,))]

    def some(at, r):
        return pl.ds(pl.multiple_of(at, 8), r)

    def rows_of(q):
        big = row_big(q)
        return [(big, (64,)), (jnp.logical_not(big), (56,))]

    def cols_of(q):
        big = col_big(q)
        return [(big, (512,)), (jnp.logical_not(big), (384,))]

    def cells_of(qx, qz):
        rb, cb = row_big(qx), col_big(qz)
        nr, nc = jnp.logical_not(rb), jnp.logical_not(cb)
        return [(rb & cb, (64, 512)), (rb & nc, (64, 384)), (nr & cb, (56, 512)), (nr & nc, (56, 384))]

    barrier = pltpu.get_barrier_semaphore()
    around = [(dy, dc) for dy in range(4) for dc in range(2) if (dy, dc) != (0, 0)]
    plane = [(dx, dz) for dx in range(4) for dz in range(4) if (dx, dz) != (0, 0)]
    at_group = [dev(x, z, ring(y + dy), lax.rem(c + dc, 2)) for dy, dc in around]
    at_plane = [dev(ring(x + dx), ring(z + dz), y, c) for dx, dz in plane]
    peers = at_group + at_plane + [dev(ring(x + d), z, y_l, c) for d in (1, 2, 3)]
    for peer in peers:
        pl.semaphore_signal(barrier, inc=1, device_id=peer, device_id_type=MESH)
    pl.semaphore_wait(barrier, len(peers))

    y_lambda, y_amps, forward = [], [], []
    for half, (j, first, n) in CUTS:
        cols = pl.ds(first, n)
        rows_l, rows_t = pl.ds(128 * half, (128, 112)[half]), pl.ds(64 * half, (64, 56)[half])
        y_lambda.append(remote(lambda j=j, r=rows_l, k=cols: l_ref.at[j, r, k], lambda j=j, r=rows_l, k=cols: lraw.at[1, j, r, k], to_l, sems.take()))
        here = lambda j=j, r=rows_t, k=cols: traw.at[2 + c, j, :, r, k]
        y_amps.append(remote(lambda j=j, r=rows_t, k=cols: t_halves.at[j, :, r, k], here, to_t, sems.take()))
        forward.append(remote(here, here, other, sems.take()))
    core_amps = [remote(lambda j=j: t_halves.at[j], lambda j=j: traw.at[c, j, :, pl.ds(0, 120), :], other, sems.take()) for j in range(2)]
    own = []
    for j in range(2):
        own.append(pltpu.make_async_copy(l_ref.at[j], lraw.at[0, j, pl.ds(0, ROWS), :], local.at[2 * j]))
        own.append(pltpu.make_async_copy(t_halves.at[j], traw.at[c, j, :, pl.ds(0, 120), :], local.at[2 * j + 1]))

    hop_l = [
        remote_sized(
            rows_of(ring(x + d)),
            lambda r, d=d: l_ref.at[:, pl.ds(row_at(ring(x + d)), r), :],
            lambda r, d=d: lx.at[d - 1, :, pl.ds(0, r), :],
            at_x(d), sems.take(),
        )
        for d in (1, 2, 3)
    ]
    hop_t = [
        remote_sized(
            cols_of(ring(z + d)),
            lambda n, d=d: t_ref.at[:, :, pl.ds(col_at(ring(z + d)), n)],
            lambda n, d=d: tz.at[d - 1, :, :, pl.ds(0, n)],
            at_z(d), sems.take(),
        )
        for d in (1, 2, 3)
    ]
    hop_s, got_s = {}, {}
    for d in (1, 2, 3):
        for q in range(4):
            s_q = sems.take()
            to = ring(z + d)
            hop_s[d, q] = remote_sized(
                shared_of(q, to),
                lambda r, q=q, to=to: t_ref.at[:, some(row_at(q) + shared_at(to), r), shared],
                lambda r, d=d, q=q, to=to: tz.at[d - 1, :, some(row_at(q) + shared_at(to), r), aside],
                at_z(d), s_q,
            )
            land = lambda r, d=d, q=q: tz.at[d - 1, :, some(row_at(q) + shared_at(z), r), aside]
            got_s[d, q] = remote_sized(shared_of(q, z), land, land, at_z(d), s_q)
    got_l = [
        remote_sized(rows_of(x), lambda r, d=d: lx.at[d - 1, :, pl.ds(0, r), :], lambda r, d=d: lx.at[d - 1, :, pl.ds(0, r), :], at_x(d), (send.at[3 * STEPS + 2 + d - 1], recv.at[3 * STEPS + 2 + d - 1]))
        for d in (1, 2, 3)
    ]
    got_t = [
        remote_sized(cols_of(z), lambda n, d=d: tz.at[d - 1, :, :, pl.ds(0, n)], lambda n, d=d: tz.at[d - 1, :, :, pl.ds(0, n)], at_z(d), (send.at[3 * STEPS + 5 + d - 1], recv.at[3 * STEPS + 5 + d - 1]))
        for d in (1, 2, 3)
    ]

    more_l, more_t, got_more_l, got_more_t, hold = {}, {}, {}, {}, {}
    second_l, second_t, got2_l, got2_t, keep_l, keep_t = {}, {}, {}, {}, {}, {}
    for d in range(4):

        def from_l(r, n, q, d=d):
            if d == 0:
                return l_ref.at[:, pl.ds(row_at(x), r), pl.ds(col_at(q), n)]
            return lx.at[d - 1, :, pl.ds(0, r), pl.ds(col_at(q), n)]

        def from_t(r, n, q, d=d):
            if d == 0:
                return t_ref.at[:, pl.ds(row_at(q), r), pl.ds(col_at(z), n)]
            return tz.at[d - 1, :, pl.ds(row_at(q), r), pl.ds(0, n)]

        def shared_l(r, q, d=d):
            if d == 0:
                return l_ref.at[:, some(row_at(x) + shared_at(q), r), shared]
            return lx.at[d - 1, :, some(shared_at(q), r), shared]

        def shared_t(r, q, d=d):
            if d == 0:
                return t_ref.at[:, some(row_at(q) + shared_at(z), r), shared]
            return tz.at[d - 1, :, some(row_at(q) + shared_at(z), r), aside]

        for e in (1, 2, 3):
            s_l, s_t = sems.take(), sems.take()
            qx, qz = ring(x + e), ring(z + e)
            more_l[d, e] = remote_sized(
                shared_of(x, qz),
                lambda r, qz=qz, f=shared_l: f(r, qz),
                lambda r, d=d, qz=qz: lz.at[ring(x - d), z, :, some(shared_at(qz), r), aside],
                at_z(e), s_l,
            )
            more_t[d, e] = remote_sized(
                shared_of(qx, z),
                lambda r, qx=qx, f=shared_t: f(r, qx),
                lambda r, d=d: tx.at[x, ring(z - d), :, some(shared_at(z), r), aside],
                at_x(e), s_t,
            )
            land_l = lambda r, d=d, e=e: lz.at[ring(x - d), ring(z - e), :, some(shared_at(z), r), aside]
            land_t = lambda r, d=d, e=e: tx.at[ring(x - e), ring(z - d), :, some(shared_at(z), r), aside]
            got_more_l[d, e] = remote_sized(shared_of(x, z), land_l, land_l, at_z(e), s_l)
            got_more_t[d, e] = remote_sized(shared_of(x, z), land_t, land_t, at_x(e), s_t)

        def hold_l(r, d=d, f=shared_l):
            return lambda: pltpu.make_async_copy(f(r, z), lz.at[ring(x - d), z, :, some(shared_at(z), r), aside], local.at[14 + d])

        def hold_t(r, d=d, f=shared_t):
            return lambda: pltpu.make_async_copy(f(r, x), tx.at[x, ring(z - d), :, some(shared_at(z), r), aside], local.at[18 + d])

        hold[d] = [Copy(*((cond, h(*size)) for cond, size in shared_of(x, z))) for h in (hold_l, hold_t)]

        for e in (1, 2, 3):
            s_l, s_t = sems.take(), sems.take()
            second_l[d, e] = remote_sized(
                cells_of(x, ring(z + e)),
                lambda r, n, d=d, e=e, f=from_l: f(r, n, ring(z + e)),
                lambda r, n, d=d: lz.at[ring(x - d), z, :, pl.ds(0, r), pl.ds(0, n)],
                at_z(e), s_l,
            )
            second_t[d, e] = remote_sized(
                cells_of(ring(x + e), z),
                lambda r, n, d=d, e=e, f=from_t: f(r, n, ring(x + e)),
                lambda r, n, d=d: tx.at[x, ring(z - d), :, pl.ds(0, r), pl.ds(0, n)],
                at_x(e), s_t,
            )
            land_l = lambda r, n, d=d, e=e: lz.at[ring(x - d), ring(z - e), :, pl.ds(0, r), pl.ds(0, n)]
            land_t = lambda r, n, d=d, e=e: tx.at[ring(x - e), ring(z - d), :, pl.ds(0, r), pl.ds(0, n)]
            got2_l[d, e] = remote_sized(cells_of(x, z), land_l, land_l, at_z(e), s_l)
            got2_t[d, e] = remote_sized(cells_of(x, z), land_t, land_t, at_x(e), s_t)

        def make_l(r, n, d=d, f=from_l):
            return lambda: pltpu.make_async_copy(f(r, n, z), lz.at[ring(x - d), z, :, pl.ds(0, r), pl.ds(0, n)], local.at[4 + d])

        def make_t(r, n, d=d, f=from_t):
            return lambda: pltpu.make_async_copy(f(r, n, x), tx.at[x, ring(z - d), :, pl.ds(0, r), pl.ds(0, n)], local.at[8 + d])

        keep_l[d] = Copy(*((cond, make_l(*size)) for cond, size in cells_of(x, z)))
        keep_t[d] = Copy(*((cond, make_t(*size)) for cond, size in cells_of(x, z)))

    pairs = pltpu.make_async_copy(pair_ref, pair_list, local.at[13])
    pairs.start()
    for copy in own:
        copy.start()
    for i in range(STEPS):
        y_lambda[i].start()
        y_amps[i].start()
        if i == 0:
            for d in (0, 2, 1):
                hop_l[d].start()
                hop_t[d].start()
                for q in range(4):
                    hop_s[d + 1, q].start()
            core_amps[0].start()
            core_amps[1].start()
    for e in (1, 3, 2):
        second_l[0, e].start()
        more_l[0, e].start()
        second_t[0, e].start()
        more_t[0, e].start()
    for copy in (keep_l[0], keep_t[0], *hold[0]):
        copy.start()

    for part in range(2):
        for j in range(2):
            lraw[part, j, ROWS:PAD, :] = jnp.zeros((PAD - ROWS, V), F32)
    for part in range(4):
        for j in range(2):
            traw[part, j, :, 120:128, :] = jnp.zeros((2, 8, V), F32)

    @pl.when(jnp.logical_not(col_big(z)))
    def _():
        empty = pl.ds(pl.multiple_of(32 - shared_at(z), 32), 32)
        lz[:, :, :, empty, aside] = jnp.zeros((4, 4, 2, 32, 128), F32)
        tx[:, :, :, empty, aside] = jnp.zeros((4, 4, 2, 32, 128), F32)

    acc[...] = jnp.zeros_like(acc)
    gram[...] = jnp.zeros_like(gram)

    def split_lanes(cut, lanes):
        j, first, n = cut

        @pl.loop(lanes[0] // 32, lanes[1] // 32)
        def _(b):
            at = pl.multiple_of(b * 32, 32)
            hi, lo = split(lraw[b // 8, j, pl.ds(pl.multiple_of((b % 8) * 32, 32), 32), pl.ds(first, n)])
            rows = pl.ds(at, 32)
            lcat[rows, 0:n] = hi
            lcat[rows, n : 2 * n] = lo
            lcat[rows, 2 * n : 3 * n] = hi

    def split_rows(cut, block, half):
        j, first, n = cut
        y_of, core = lax.div(block, 2), lax.rem(block, 2)

        @pl.loop(0, 4)
        def _(b):
            at = pl.multiple_of((b % 2) * 32, 32)
            hi, lo = split(traw[block, j, b // 2, pl.ds(64 * half + at, 32), pl.ds(first, n)])
            rows = pl.ds(pl.multiple_of(y_of * 512 + half * 256 + core * 128 + b * 32, 32), 32)
            tcat[rows, 0:n] = hi
            tcat[rows, n : 2 * n] = hi
            tcat[rows, 2 * n : 3 * n] = lo

    def multiply(cut, y_of, half, lanes, core=None):
        n = cut[2]
        at = y_of * 512 + half * 256
        span = pl.ds(at, 256) if core is None else pl.ds(pl.multiple_of(at + core * 128, 128), 128)
        for lane in range(*lanes, 128 if lanes[1] - lanes[0] == 128 else 256):
            wide = min(256, lanes[1] - lane)
            r = dot_nt(tcat[span, 0 : 3 * n], lcat[lane : lane + wide, 0 : 3 * n])
            if core is None:
                acc[y_of, half, :, :, :, lane : lane + wide] += r.reshape(4, 2, 32, wide)
            else:
                acc[y_of, half, pl.ds(2 * core, 2), :, :, lane : lane + wide] += r.reshape(2, 2, 32, wide)

    def part_of(q):
        return pl.ds(pl.multiple_of(8 * q, 8), 8)

    firsts, second = {0: ([], []), 1: ([], []), 2: ([], [])}, ({}, {})
    pieces = (
        (0, 0, None, 0, 256),
        (1, 0, None, 256, 128), (1, 1, 0, 0, 384),
        (2, 0, None, 384, 128), (2, 1, 0, 384, 128), (2, 1, 1, 0, 512),
    )
    for when, b, half, lane, wide in pieces:
        lanes = pl.ds(lane, wide)
        for d in (1, 3, 2):
            qx, qz = ring(x + d), ring(z + d)

            def src_z(b=b, half=half, lanes=lanes, qz=qz):
                return acc.at[b, :, qz, 0, :, lanes] if half is None else acc.at[b, half, qz, 0, :, lanes]

            def dst_z(b=b, half=half, lanes=lanes, d=d):
                return rz1.at[d - 1, b, :, :, lanes] if half is None else rz1.at[d - 1, b, half, :, lanes]

            def src_x(b=b, half=half, lanes=lanes, qx=qx):
                return acc.at[b, :, :, 1, part_of(qx), lanes] if half is None else acc.at[b, half, :, 1, part_of(qx), lanes]

            def dst_x(b=b, half=half, lanes=lanes, d=d):
                return rx1.at[d - 1, b, :, :, :, lanes] if half is None else rx1.at[d - 1, b, half, :, :, lanes]

            firsts[when][b].append(remote(src_z, dst_z, at_z(d), sems.take()))
            firsts[when][b].append(remote(src_x, dst_x, at_x(d), sems.take()))
    for d in (1, 3, 2):
        qx, qz = ring(x + d), ring(z + d)
        for b in range(2):
            second[b]["z", d] = remote(lambda qx=qx, b=b: sz.at[b, :, part_of(qx), :], lambda d=d, b=b: rz2.at[d - 1, b], at_x(d), sems.take())
            second[b]["x", d] = remote(lambda qz=qz, b=b: sx.at[b, :, qz], lambda d=d, b=b: rx2.at[d - 1, b], at_z(d), sems.take())

    for copy in own:
        copy.wait()
    for k, one in enumerate(WIDE):
        split_lanes(one, (0, 256))
        if k % 3 == 0:
            core_amps[one[0]].wait_recv()
        for half in range(2):
            pl.loop(0, 2)(lambda block, half=half: split_rows(one, block, half))
            multiply(one, 0, half, (0, 256))
    for i in range(STEPS):
        now, one = CUTS[i]
        fresh = (256 + 128 * now, 384 + 128 * now)
        split_lanes(one, (0, 256 + 128 * now))
        for half in range(2):
            pl.loop(0, 2 + 2 * (half < now))(lambda block, half=half: split_rows(one, block, half))
        y_amps[i].wait_recv()
        forward[i].start()
        split_rows(one, 2 + c, now)
        y_lambda[i].wait_recv()
        split_lanes(one, fresh)
        for half in range(2):
            multiply(one, 0, half, fresh)
        if i == STEPS - 1:
            for copy in firsts[2][0]:
                copy.start()
        if now == 1:
            multiply(one, 1, 0, fresh)
        multiply(one, 1, now, (0, fresh[1]), c)
        forward[i].wait_recv()
        split_rows(one, 3 - c, now)
        multiply(one, 1, now, (0, fresh[1]), 1 - c)
        if i == STEPS - 3:
            for copy in firsts[0][0] + firsts[1][0] + firsts[1][1]:
                copy.start()
        if i == 5:
            for d in (1, 3, 2):
                got_l[d - 1].wait_recv()
                for e in (1, 3, 2):
                    second_l[d, e].start()
                    more_l[d, e].start()
                keep_l[d].start()
                got_t[d - 1].wait_recv()
                for q in range(4):
                    got_s[d, q].wait_recv()
                for e in (1, 3, 2):
                    second_t[d, e].start()
                    more_t[d, e].start()
                keep_t[d].start()
                for copy in hold[d]:
                    copy.start()
    for copy in firsts[2][1]:
        copy.start()

    for d in range(4):
        keep_l[d].wait()
        keep_t[d].wait()
        for copy in hold[d]:
            copy.wait()
        for e in (1, 2, 3):
            for came in (got2_l, got2_t, got_more_l, got_more_t):
                came[d, e].wait_recv()
    @pl.loop(0, jnp.where(row_big(x), 8, 7))
    def _(b):
        rows = pl.ds(pl.multiple_of(b * 8, 8), 8)
        a_hi, a_lo = split(lz[:, :, :, rows, :].reshape(256, 512))
        b_hi, b_lo = split(tx[:, :, :, rows, :].reshape(256, 512))
        gram[...] += dot_nt(a_hi, b_hi) + (dot_nt(a_lo, b_hi) + dot_nt(a_hi, b_lo))

    row = lax.broadcasted_iota(jnp.int32, (256, 256), 0)
    col = lax.broadcasted_iota(jnp.int32, (256, 256), 1)
    same = lax.rem(row, 8) == lax.rem(col, 8)
    by_row = jnp.where(same, gram[...], 0.0).reshape(NP, 8, 256).sum(axis=1)
    pick = lax.broadcasted_iota(jnp.int32, (256, 128), 0)
    lane = lax.broadcasted_iota(jnp.int32, (256, 128), 1)
    inter = jnp.zeros((8, 128), F32)
    for k in range(4):
        wanted = (lax.div(pick, 8) + 32 * k == lane).astype(F32)
        inter += lax.dot_general(by_row[8 * k : 8 * k + 8], wanted, (((1,), (0,)), ((), ())), precision=lax.Precision.HIGHEST, preferred_element_type=F32)

    def share(buf, me, places, value):
        buf[me] = value
        copies = [remote(lambda: buf.at[me], lambda: buf.at[me], place, sems.take()) for place in places]
        for copy in copies:
            copy.start()
        return copies

    def total(buf, copies, n):
        for copy in copies:
            copy.wait_recv()
        value = buf[0]
        for k in range(1, n):
            value = value + buf[k]
        return value

    over_group = share(ig, virt, at_group, inter)

    def sum_first(b):
        for when in firsts.values():
            for copy in when[b]:
                copy.wait_recv()
        for half in range(2):
            sz[b, half] = (acc[b, half, z, 0] + rz1[0, b, half]) + (rz1[1, b, half] + rz1[2, b, half])
        for d in (1, 3, 2):
            second[b]["z", d].start()
        for half in range(2):
            sx[b, half] = (acc[b, half, :, 1, part_of(x), :] + rx1[0, b, half]) + (rx1[1, b, half] + rx1[2, b, half])
        for d in (1, 3, 2):
            second[b]["x", d].start()

    lasts = []

    def sum_second(b):
        for copy in second[b].values():
            copy.wait_recv()
        for half in range(2):
            done[b, half, 0] = (sz[b, half, part_of(x), :] + rz2[0, b, half]) + (rz2[1, b, half] + rz2[2, b, half])
            done[b, half, 1] = (sx[b, half, z] + rx2[0, b, half]) + (rx2[1, b, half] + rx2[2, b, half])
        q = (y, y_t)[b]
        for h in range(2):
            s = sems.take()[0]
            block = lambda h=h: done.at[b, :, :, :, pl.ds(256 * h, 256)]
            make = lambda h=h, s=s, block=block: pltpu.make_async_remote_copy(src_ref=block(), dst_ref=fin.at[:, :, x], send_sem=s, recv_sem=recv.at[N_SEMS - 4 + x], device_id=dev(q, z, (y, y_l)[h], c), device_id_type=MESH)
            if h == 0:
                go = Copy((q != x, make))
                stay = Copy((q == x, lambda block=block: pltpu.make_async_copy(block(), fin.at[:, :, x], local.at[12])))
                stay.start()
            else:
                go, stay = Copy((None, make)), Copy()
            go.start()
            lasts.append((go, stay))

    sum_first(0)
    over_plane = share(ip, pair, at_plane, total(ig, over_group, 8))
    sum_first(1)
    sum_second(0)
    sum_second(1)

    every = total(ip, over_plane, 16)
    matrix = jnp.concatenate([every[:, 32 * k : 32 * k + 32] for k in range(4)], axis=0)
    pairs.wait()
    first, kind = pair_list[0:1, :], pair_list[1:2, :]
    one_hot = (first == lax.broadcasted_iota(jnp.int32, (256, NP), 0)).astype(F32)
    kind = (kind == lax.broadcasted_iota(jnp.int32, (NP, NP), 0)).astype(F32)
    same_k = lax.dot_general(kind, kind, (((0,), (0,)), ((), ())), preferred_element_type=F32)
    highest = lax.Precision.HIGHEST
    outer = lax.dot_general(one_hot, same_k * matrix, (((1,), (0,)), ((), ())), precision=highest, preferred_element_type=F32)
    occ_ref[...] = -lax.dot_general(outer, one_hot, NT, precision=highest, preferred_element_type=F32)[:OCC]

    for go, stay in lasts:
        stay.wait()
    in_plane = (x == y) | (x == y_t)
    for q in range(4):
        came = Copy((jnp.logical_not(in_plane & (x == q)), lambda q=q: pltpu.make_async_remote_copy(src_ref=fin.at[:, :, q], dst_ref=fin.at[:, :, q], send_sem=send.at[0], recv_sem=recv.at[N_SEMS - 4 + q], device_id=to_l, device_id_type=MESH)))
        came.wait_recv()

    sent = y_lambda + y_amps + forward + core_amps + hop_l + hop_t + list(second_l.values()) + list(second_t.values())
    for group in (hop_s, more_l, more_t):
        sent += list(group.values())
    sent += [copy for when in firsts.values() for one in when for copy in one] + list(second[0].values()) + list(second[1].values()) + [go for go, _ in lasts] + over_group + over_plane
    for copy in sent:
        copy.wait_send()


def finish(fin_ref, occ_in, virt_ref, occ_ref):
    virt_ref[...] = fin_ref[...].reshape(128, 256).T[:ROWS, :120]
    occ_ref[...] = occ_in[:, :OCC]


def shards(lambda_blocks, amplitudes, pair_list):
    vmem = lambda shape, dtype=F32: pltpu.VMEM(shape, dtype)
    fin, occ = pl.pallas_call(
        kernel,
        out_shape=(jax.ShapeDtypeStruct((2, 2, 4, 8, 256), F32), jax.ShapeDtypeStruct((OCC, 256), F32)),
        in_specs=[pl.BlockSpec(memory_space=pl.ANY)] * 4,
        out_specs=(pl.BlockSpec(memory_space=pl.ANY), pl.BlockSpec(memory_space=pltpu.VMEM)),
        scratch_shapes=[
            vmem((2, 2, PAD, V)), vmem((4, 2, 2, 128, V)), vmem((512, 3 * KC), BF16), vmem((1024, 3 * KC), BF16), vmem((2, 2, 4, 2, 32, 512)),
            vmem((3, 2, 64, V)), vmem((3, 2, ROWS, 512)), vmem((4, 4, 2, 64, 512)), vmem((4, 4, 2, 64, 512)), vmem((256, 256)),
            vmem((3, 2, 2, 32, 512)), vmem((3, 2, 2, 4, 8, 512)), vmem((3, 2, 2, 8, 512)), vmem((3, 2, 2, 8, 512)),
            vmem((2, 2, 32, 512)), vmem((2, 2, 4, 8, 512)), vmem((2, 2, 2, 8, 512)), vmem((8, 8, 128)), vmem((16, 8, 128)), vmem((2, NP), jnp.int32),
            pltpu.SemaphoreType.DMA((N_SEMS,)), pltpu.SemaphoreType.DMA((N_SEMS,)), pltpu.SemaphoreType.DMA((22,)),
        ],
        compiler_params=pltpu.CompilerParams(collective_id=0, has_side_effects=True, vmem_limit_bytes=60 * 2**20),
        cost_estimate=pl.CostEstimate(flops=12_000_000_000, bytes_accessed=8_000_000, transcendentals=0),
    )(lambda_blocks, amplitudes, amplitudes.reshape(2, 2, 120, V), pair_list.T)
    return pl.pallas_call(
        finish,
        out_shape=(jax.ShapeDtypeStruct((ROWS, 120), F32), jax.ShapeDtypeStruct((OCC, OCC), F32)),
        in_specs=[pl.BlockSpec(memory_space=pltpu.VMEM)] * 2,
        out_specs=(pl.BlockSpec(memory_space=pltpu.VMEM),) * 2,
    )(fin, occ)


def solution(mesh):
    in_specs = (P("pair", "virt", None), P("pair", "virt", None), P())
    out_specs = (P("virt", "pair"), P())
    return jax.shard_map(shards, mesh=mesh, in_specs=in_specs, out_specs=out_specs, check_vma=False)
```

```python
import jax
import jax.numpy as jnp
from jax import lax
from jax.experimental import pallas as pl
from jax.experimental.pallas import tpu as pltpu
from jax.sharding import PartitionSpec as P

OCC = 200
NP = 32
ROWS = 240
PAD = 256
V = 1920
WIDE = ((0, 0, 640), (0, 640, 640), (0, 1280, 640), (1, 0, 640), (1, 640, 640), (1, 1280, 640))
NARROW = WIDE[:5] + ((1, 1280, 384), (1, 1664, 256))
CUTS = tuple((0, cut) for cut in WIDE) + tuple((1, cut) for cut in NARROW)
KC = 640
STEPS = len(CUTS)
MESH = pl.DeviceIdType.MESH
F32 = jnp.float32
BF16 = jnp.bfloat16


class Copy:
    def __init__(self, *variants):
        self.variants = variants

    def _each(self, act):
        for cond, make in self.variants:
            if cond is None:
                act(make())
            else:

                @pl.when(cond)
                def _(make=make):
                    act(make())

    def start(self):
        self._each(lambda c: c.start())

    def wait_send(self):
        self._each(lambda c: c.wait_send())

    def wait_recv(self):
        self._each(lambda c: c.wait_recv())

    def wait(self):
        self._each(lambda c: c.wait())


class Sems:
    def __init__(self, send, recv):
        self.send, self.recv, self.n = send, recv, 0

    def take(self):
        self.n += 1
        return self.send.at[self.n - 1], self.recv.at[self.n - 1]


def split(v):
    hi = v.astype(BF16)
    return hi, (v - hi.astype(F32)).astype(BF16)


NT = (((1,), (1,)), ((), ()))


def dot_nt(a, b):
    return lax.dot_general(a, b, NT, preferred_element_type=F32)


N_SEMS = 224


def kernel(
    l_ref, t_ref, t_halves, pair_ref, fin, occ_ref,
    lraw, traw, lcat, tcat, acc, lx, tz, lz, tx, gram,
    rz1, rx1, rz2, rx2, sz, sx, done, ig, ip, pair_list,
    send, recv, local,
):
    pair, virt = lax.axis_index("pair"), lax.axis_index("virt")
    x, z = lax.div(pair, 4), lax.rem(pair, 4)
    y, c = lax.div(virt, 2), lax.rem(virt, 2)
    sems = Sems(send, recv)

    def ring(a):
        return lax.rem(a + 4, 4)

    def dev(xx, zz, yy, cc):
        return (xx * 4 + zz, yy * 2 + cc)

    def at_x(d):
        return dev(ring(x + d), z, y, c)

    def at_z(d):
        return dev(x, ring(z + d), y, c)

    def at_y(d):
        return dev(x, z, ring(y + d), c)

    other = dev(x, z, y, 1 - c)
    y_l = y + 1 - 2 * lax.rem(y, 2)
    y_t = 3 - y
    to_l, to_t = dev(x, z, y_l, c), dev(x, z, y_t, c)

    def remote(src, dst, device, pair_of_sems):
        s, r = pair_of_sems
        return Copy((None, lambda: pltpu.make_async_remote_copy(src_ref=src(), dst_ref=dst(), send_sem=s, recv_sem=r, device_id=device, device_id_type=MESH)))

    def remote_sized(shapes, src, dst, device, pair_of_sems):
        s, r = pair_of_sems

        def make(size):
            return lambda: pltpu.make_async_remote_copy(src_ref=src(*size), dst_ref=dst(*size), send_sem=s, recv_sem=r, device_id=device, device_id_type=MESH)

        return Copy(*((cond, make(size)) for cond, size in shapes))

    def row_big(q):
        return (q < 2) == (c == 0)

    def row_at(q):
        return pl.multiple_of(56 * q + 8 * jnp.where(c == 0, jnp.minimum(q, 2), jnp.maximum(q - 2, 0)), 8)

    def col_big(q):
        return lax.div(q, 2) != c

    def col_at(q):
        return pl.multiple_of(512 * q - 128 * jnp.where((c == 0) & (q > 1), 1, 0), 128)

    shared = pl.ds(pl.multiple_of(384 + 1024 * c, 128), 128)
    aside = pl.ds(384, 128)

    def shared_at(q):
        return 32 * (1 - lax.rem(q, 2))

    def shared_of(qx, qz):
        short, odd, big = jnp.logical_not(col_big(qz)), lax.rem(qz, 2) == 1, row_big(qx)
        narrow = jnp.logical_not(odd) & jnp.logical_not(big)
        return [(short & jnp.logical_not(narrow), (32,)), (short & narrow, (24,))]

    def some(at, r):
        return pl.ds(pl.multiple_of(at, 8), r)

    def rows_of(q):
        big = row_big(q)
        return [(big, (64,)), (jnp.logical_not(big), (56,))]

    def cols_of(q):
        big = col_big(q)
        return [(big, (512,)), (jnp.logical_not(big), (384,))]

    def cells_of(qx, qz):
        rb, cb = row_big(qx), col_big(qz)
        nr, nc = jnp.logical_not(rb), jnp.logical_not(cb)
        return [(rb & cb, (64, 512)), (rb & nc, (64, 384)), (nr & cb, (56, 512)), (nr & nc, (56, 384))]

    barrier = pltpu.get_barrier_semaphore()
    around = [(dy, dc) for dy in range(4) for dc in range(2) if (dy, dc) != (0, 0)]
    plane = [(dx, dz) for dx in range(4) for dz in range(4) if (dx, dz) != (0, 0)]
    at_group = [dev(x, z, ring(y + dy), lax.rem(c + dc, 2)) for dy, dc in around]
    at_plane = [dev(ring(x + dx), ring(z + dz), y, c) for dx, dz in plane]
    peers = at_group + at_plane + [dev(ring(x + d), z, y_l, c) for d in (1, 2, 3)]
    for peer in peers:
        pl.semaphore_signal(barrier, inc=1, device_id=peer, device_id_type=MESH)
    pl.semaphore_wait(barrier, len(peers))

    y_lambda, y_amps, forward = [], [], []
    for half, (j, first, n) in CUTS:
        cols = pl.ds(first, n)
        rows_l, rows_t = pl.ds(128 * half, (128, 112)[half]), pl.ds(64 * half, (64, 56)[half])
        y_lambda.append(remote(lambda j=j, r=rows_l, k=cols: l_ref.at[j, r, k], lambda j=j, r=rows_l, k=cols: lraw.at[1, j, r, k], to_l, sems.take()))
        here = lambda j=j, r=rows_t, k=cols: traw.at[2 + c, j, :, r, k]
        y_amps.append(remote(lambda j=j, r=rows_t, k=cols: t_halves.at[j, :, r, k], here, to_t, sems.take()))
        forward.append(remote(here, here, other, sems.take()))
    core_amps = [remote(lambda j=j: t_halves.at[j], lambda j=j: traw.at[c, j, :, pl.ds(0, 120), :], other, sems.take()) for j in range(2)]
    own = []
    for j in range(2):
        own.append(pltpu.make_async_copy(l_ref.at[j], lraw.at[0, j, pl.ds(0, ROWS), :], local.at[2 * j]))
        own.append(pltpu.make_async_copy(t_halves.at[j], traw.at[c, j, :, pl.ds(0, 120), :], local.at[2 * j + 1]))

    hop_l = [
        remote_sized(
            rows_of(ring(x + d)),
            lambda r, d=d: l_ref.at[:, pl.ds(row_at(ring(x + d)), r), :],
            lambda r, d=d: lx.at[d - 1, :, pl.ds(0, r), :],
            at_x(d), sems.take(),
        )
        for d in (1, 2, 3)
    ]
    hop_t = [
        remote_sized(
            cols_of(ring(z + d)),
            lambda n, d=d: t_ref.at[:, :, pl.ds(col_at(ring(z + d)), n)],
            lambda n, d=d: tz.at[d - 1, :, :, pl.ds(0, n)],
            at_z(d), sems.take(),
        )
        for d in (1, 2, 3)
    ]
    hop_s, got_s = {}, {}
    for d in (1, 2, 3):
        for q in range(4):
            s_q = sems.take()
            to = ring(z + d)
            hop_s[d, q] = remote_sized(
                shared_of(q, to),
                lambda r, q=q, to=to: t_ref.at[:, some(row_at(q) + shared_at(to), r), shared],
                lambda r, d=d, q=q, to=to: tz.at[d - 1, :, some(row_at(q) + shared_at(to), r), aside],
                at_z(d), s_q,
            )
            land = lambda r, d=d, q=q: tz.at[d - 1, :, some(row_at(q) + shared_at(z), r), aside]
            got_s[d, q] = remote_sized(shared_of(q, z), land, land, at_z(d), s_q)
    got_l = [
        remote_sized(rows_of(x), lambda r, d=d: lx.at[d - 1, :, pl.ds(0, r), :], lambda r, d=d: lx.at[d - 1, :, pl.ds(0, r), :], at_x(d), (send.at[3 * STEPS + 2 + d - 1], recv.at[3 * STEPS + 2 + d - 1]))
        for d in (1, 2, 3)
    ]
    got_t = [
        remote_sized(cols_of(z), lambda n, d=d: tz.at[d - 1, :, :, pl.ds(0, n)], lambda n, d=d: tz.at[d - 1, :, :, pl.ds(0, n)], at_z(d), (send.at[3 * STEPS + 5 + d - 1], recv.at[3 * STEPS + 5 + d - 1]))
        for d in (1, 2, 3)
    ]

    more_l, more_t, got_more_l, got_more_t, hold = {}, {}, {}, {}, {}
    second_l, second_t, got2_l, got2_t, keep_l, keep_t = {}, {}, {}, {}, {}, {}
    for d in range(4):

        def from_l(r, n, q, d=d):
            if d == 0:
                return l_ref.at[:, pl.ds(row_at(x), r), pl.ds(col_at(q), n)]
            return lx.at[d - 1, :, pl.ds(0, r), pl.ds(col_at(q), n)]

        def from_t(r, n, q, d=d):
            if d == 0:
                return t_ref.at[:, pl.ds(row_at(q), r), pl.ds(col_at(z), n)]
            return tz.at[d - 1, :, pl.ds(row_at(q), r), pl.ds(0, n)]

        def shared_l(r, q, d=d):
            if d == 0:
                return l_ref.at[:, some(row_at(x) + shared_at(q), r), shared]
            return lx.at[d - 1, :, some(shared_at(q), r), shared]

        def shared_t(r, q, d=d):
            if d == 0:
                return t_ref.at[:, some(row_at(q) + shared_at(z), r), shared]
            return tz.at[d - 1, :, some(row_at(q) + shared_at(z), r), aside]

        for e in (1, 2, 3):
            s_l, s_t = sems.take(), sems.take()
            qx, qz = ring(x + e), ring(z + e)
            more_l[d, e] = remote_sized(
                shared_of(x, qz),
                lambda r, qz=qz, f=shared_l: f(r, qz),
                lambda r, d=d, qz=qz: lz.at[ring(x - d), z, :, some(shared_at(qz), r), aside],
                at_z(e), s_l,
            )
            more_t[d, e] = remote_sized(
                shared_of(qx, z),
                lambda r, qx=qx, f=shared_t: f(r, qx),
                lambda r, d=d: tx.at[x, ring(z - d), :, some(shared_at(z), r), aside],
                at_x(e), s_t,
            )
            land_l = lambda r, d=d, e=e: lz.at[ring(x - d), ring(z - e), :, some(shared_at(z), r), aside]
            land_t = lambda r, d=d, e=e: tx.at[ring(x - e), ring(z - d), :, some(shared_at(z), r), aside]
            got_more_l[d, e] = remote_sized(shared_of(x, z), land_l, land_l, at_z(e), s_l)
            got_more_t[d, e] = remote_sized(shared_of(x, z), land_t, land_t, at_x(e), s_t)

        def hold_l(r, d=d, f=shared_l):
            return lambda: pltpu.make_async_copy(f(r, z), lz.at[ring(x - d), z, :, some(shared_at(z), r), aside], local.at[14 + d])

        def hold_t(r, d=d, f=shared_t):
            return lambda: pltpu.make_async_copy(f(r, x), tx.at[x, ring(z - d), :, some(shared_at(z), r), aside], local.at[18 + d])

        hold[d] = [Copy(*((cond, h(*size)) for cond, size in shared_of(x, z))) for h in (hold_l, hold_t)]

        for e in (1, 2, 3):
            s_l, s_t = sems.take(), sems.take()
            second_l[d, e] = remote_sized(
                cells_of(x, ring(z + e)),
                lambda r, n, d=d, e=e, f=from_l: f(r, n, ring(z + e)),
                lambda r, n, d=d: lz.at[ring(x - d), z, :, pl.ds(0, r), pl.ds(0, n)],
                at_z(e), s_l,
            )
            second_t[d, e] = remote_sized(
                cells_of(ring(x + e), z),
                lambda r, n, d=d, e=e, f=from_t: f(r, n, ring(x + e)),
                lambda r, n, d=d: tx.at[x, ring(z - d), :, pl.ds(0, r), pl.ds(0, n)],
                at_x(e), s_t,
            )
            land_l = lambda r, n, d=d, e=e: lz.at[ring(x - d), ring(z - e), :, pl.ds(0, r), pl.ds(0, n)]
            land_t = lambda r, n, d=d, e=e: tx.at[ring(x - e), ring(z - d), :, pl.ds(0, r), pl.ds(0, n)]
            got2_l[d, e] = remote_sized(cells_of(x, z), land_l, land_l, at_z(e), s_l)
            got2_t[d, e] = remote_sized(cells_of(x, z), land_t, land_t, at_x(e), s_t)

        def make_l(r, n, d=d, f=from_l):
            return lambda: pltpu.make_async_copy(f(r, n, z), lz.at[ring(x - d), z, :, pl.ds(0, r), pl.ds(0, n)], local.at[4 + d])

        def make_t(r, n, d=d, f=from_t):
            return lambda: pltpu.make_async_copy(f(r, n, x), tx.at[x, ring(z - d), :, pl.ds(0, r), pl.ds(0, n)], local.at[8 + d])

        keep_l[d] = Copy(*((cond, make_l(*size)) for cond, size in cells_of(x, z)))
        keep_t[d] = Copy(*((cond, make_t(*size)) for cond, size in cells_of(x, z)))

    pairs = pltpu.make_async_copy(pair_ref, pair_list, local.at[13])
    pairs.start()
    for copy in own:
        copy.start()
    for i in range(STEPS):
        y_lambda[i].start()
        y_amps[i].start()
        if i == 0:
            for d in (0, 2, 1):
                hop_l[d].start()
                hop_t[d].start()
                for q in range(4):
                    hop_s[d + 1, q].start()
            core_amps[0].start()
            core_amps[1].start()
    for e in (1, 3, 2):
        second_l[0, e].start()
        more_l[0, e].start()
        second_t[0, e].start()
        more_t[0, e].start()
    for copy in (keep_l[0], keep_t[0], *hold[0]):
        copy.start()

    for part in range(2):
        for j in range(2):
            lraw[part, j, ROWS:PAD, :] = jnp.zeros((PAD - ROWS, V), F32)
    for part in range(4):
        for j in range(2):
            traw[part, j, :, 120:128, :] = jnp.zeros((2, 8, V), F32)

    @pl.when(jnp.logical_not(col_big(z)))
    def _():
        empty = pl.ds(pl.multiple_of(32 - shared_at(z), 32), 32)
        lz[:, :, :, empty, aside] = jnp.zeros((4, 4, 2, 32, 128), F32)
        tx[:, :, :, empty, aside] = jnp.zeros((4, 4, 2, 32, 128), F32)

    acc[...] = jnp.zeros_like(acc)
    gram[...] = jnp.zeros_like(gram)

    def split_lanes(cut, lanes):
        j, first, n = cut

        @pl.loop(lanes[0] // 32, lanes[1] // 32)
        def _(b):
            at = pl.multiple_of(b * 32, 32)
            hi, lo = split(lraw[b // 8, j, pl.ds(pl.multiple_of((b % 8) * 32, 32), 32), pl.ds(first, n)])
            rows = pl.ds(at, 32)
            lcat[rows, 0:n] = hi
            lcat[rows, n : 2 * n] = lo
            lcat[rows, 2 * n : 3 * n] = hi

    def split_rows(cut, block, half):
        j, first, n = cut
        y_of, core = lax.div(block, 2), lax.rem(block, 2)

        @pl.loop(0, 4)
        def _(b):
            at = pl.multiple_of((b % 2) * 32, 32)
            hi, lo = split(traw[block, j, b // 2, pl.ds(64 * half + at, 32), pl.ds(first, n)])
            rows = pl.ds(pl.multiple_of(y_of * 512 + half * 256 + core * 128 + b * 32, 32), 32)
            tcat[rows, 0:n] = hi
            tcat[rows, n : 2 * n] = hi
            tcat[rows, 2 * n : 3 * n] = lo

    def multiply(cut, y_of, half, lanes, core=None):
        n = cut[2]
        at = y_of * 512 + half * 256
        span = pl.ds(at, 256) if core is None else pl.ds(pl.multiple_of(at + core * 128, 128), 128)
        for lane in range(*lanes, 128 if lanes[1] - lanes[0] == 128 else 256):
            wide = min(256, lanes[1] - lane)
            r = dot_nt(tcat[span, 0 : 3 * n], lcat[lane : lane + wide, 0 : 3 * n])
            if core is None:
                acc[y_of, half, :, :, :, lane : lane + wide] += r.reshape(4, 2, 32, wide)
            else:
                acc[y_of, half, pl.ds(2 * core, 2), :, :, lane : lane + wide] += r.reshape(2, 2, 32, wide)

    def part_of(q):
        return pl.ds(pl.multiple_of(8 * q, 8), 8)

    firsts, second = {0: ([], []), 1: ([], []), 2: ([], [])}, {}
    groups = {(b, h): [] for b in range(2) for h in range(2)}
    pieces = (
        (0, 0, None, 0, 256),
        (1, 0, None, 256, 128), (1, 1, 0, 0, 256), (1, 1, 0, 256, 128),
        (2, 0, None, 384, 128), (2, 1, 1, 0, 256), (2, 1, 0, 384, 128), (2, 1, 1, 256, 256),
    )
    for when, b, half, lane, wide in pieces:
        lanes = pl.ds(lane, wide)
        for d in (1, 3, 2):
            qx, qz = ring(x + d), ring(z + d)

            def src_z(b=b, half=half, lanes=lanes, qz=qz):
                return acc.at[b, :, qz, 0, :, lanes] if half is None else acc.at[b, half, qz, 0, :, lanes]

            def dst_z(b=b, half=half, lanes=lanes, d=d):
                return rz1.at[d - 1, b, :, :, lanes] if half is None else rz1.at[d - 1, b, half, :, lanes]

            def src_x(b=b, half=half, lanes=lanes, qx=qx):
                return acc.at[b, :, :, 1, part_of(qx), lanes] if half is None else acc.at[b, half, :, 1, part_of(qx), lanes]

            def dst_x(b=b, half=half, lanes=lanes, d=d):
                return rx1.at[d - 1, b, :, :, :, lanes] if half is None else rx1.at[d - 1, b, half, :, :, lanes]

            both = [remote(src_z, dst_z, at_z(d), sems.take()), remote(src_x, dst_x, at_x(d), sems.take())]
            firsts[when][b].extend(both)
            groups[b, lane // 256].extend(both)
    for d in (1, 3, 2):
        qx, qz = ring(x + d), ring(z + d)
        for b, h in groups:
            lanes = pl.ds(256 * h, 256)
            second[b, h, "z", d] = remote(lambda qx=qx, b=b, k=lanes: sz.at[b, :, part_of(qx), k], lambda d=d, b=b, k=lanes: rz2.at[d - 1, b, :, :, k], at_x(d), sems.take())
            second[b, h, "x", d] = remote(lambda qz=qz, b=b, k=lanes: sx.at[b, :, qz, :, k], lambda d=d, b=b, k=lanes: rx2.at[d - 1, b, :, :, k], at_z(d), sems.take())

    for copy in own:
        copy.wait()
    for k, one in enumerate(WIDE):
        split_lanes(one, (0, 256))
        if k % 3 == 0:
            core_amps[one[0]].wait_recv()
        for half in range(2):
            pl.loop(0, 2)(lambda block, half=half: split_rows(one, block, half))
            multiply(one, 0, half, (0, 256))
    for i in range(STEPS):
        now, one = CUTS[i]
        fresh = (256 + 128 * now, 384 + 128 * now)
        split_lanes(one, (0, 256 + 128 * now))
        for half in range(2):
            pl.loop(0, 2 + 2 * (half < now))(lambda block, half=half: split_rows(one, block, half))
        y_amps[i].wait_recv()
        forward[i].start()
        split_rows(one, 2 + c, now)
        y_lambda[i].wait_recv()
        split_lanes(one, fresh)
        for half in range(2):
            multiply(one, 0, half, fresh)
        if i == STEPS - 1:
            for copy in firsts[2][0]:
                copy.start()
        if now == 1:
            multiply(one, 1, 0, fresh)
        multiply(one, 1, now, (0, fresh[1]), c)
        forward[i].wait_recv()
        split_rows(one, 3 - c, now)
        multiply(one, 1, now, (0, fresh[1]), 1 - c)
        if i == STEPS - 3:
            for copy in firsts[0][0] + firsts[1][0] + firsts[1][1]:
                copy.start()
        if i == 5:
            for d in (1, 3, 2):
                got_l[d - 1].wait_recv()
                for e in (1, 3, 2):
                    second_l[d, e].start()
                    more_l[d, e].start()
                keep_l[d].start()
                got_t[d - 1].wait_recv()
                for q in range(4):
                    got_s[d, q].wait_recv()
                for e in (1, 3, 2):
                    second_t[d, e].start()
                    more_t[d, e].start()
                keep_t[d].start()
                for copy in hold[d]:
                    copy.start()
    for copy in firsts[2][1]:
        copy.start()

    for d in range(4):
        keep_l[d].wait()
        keep_t[d].wait()
        for copy in hold[d]:
            copy.wait()
        for e in (1, 2, 3):
            for came in (got2_l, got2_t, got_more_l, got_more_t):
                came[d, e].wait_recv()
    @pl.loop(0, jnp.where(row_big(x), 8, 7))
    def _(b):
        rows = pl.ds(pl.multiple_of(b * 8, 8), 8)
        a_hi, a_lo = split(lz[:, :, :, rows, :].reshape(256, 512))
        b_hi, b_lo = split(tx[:, :, :, rows, :].reshape(256, 512))
        gram[...] += dot_nt(a_hi, b_hi) + (dot_nt(a_lo, b_hi) + dot_nt(a_hi, b_lo))

    row = lax.broadcasted_iota(jnp.int32, (256, 256), 0)
    col = lax.broadcasted_iota(jnp.int32, (256, 256), 1)
    same = lax.rem(row, 8) == lax.rem(col, 8)
    by_row = jnp.where(same, gram[...], 0.0).reshape(NP, 8, 256).sum(axis=1)
    pick = lax.broadcasted_iota(jnp.int32, (256, 128), 0)
    lane = lax.broadcasted_iota(jnp.int32, (256, 128), 1)
    inter = jnp.zeros((8, 128), F32)
    for k in range(4):
        wanted = (lax.div(pick, 8) + 32 * k == lane).astype(F32)
        inter += lax.dot_general(by_row[8 * k : 8 * k + 8], wanted, (((1,), (0,)), ((), ())), precision=lax.Precision.HIGHEST, preferred_element_type=F32)

    def share(buf, me, places, value):
        buf[me] = value
        copies = [remote(lambda: buf.at[me], lambda: buf.at[me], place, sems.take()) for place in places]
        for copy in copies:
            copy.start()
        return copies

    def total(buf, copies, n):
        for copy in copies:
            copy.wait_recv()
        value = buf[0]
        for k in range(1, n):
            value = value + buf[k]
        return value

    over_group = share(ig, virt, at_group, inter)

    def sum_first(b, h):
        for copy in groups[b, h]:
            copy.wait_recv()
        k = pl.ds(256 * h, 256)
        for half in range(2):
            sz[b, half, :, k] = (acc[b, half, z, 0, :, k] + rz1[0, b, half, :, k]) + (rz1[1, b, half, :, k] + rz1[2, b, half, :, k])
        for d in (1, 3, 2):
            second[b, h, "z", d].start()
        for half in range(2):
            sx[b, half, :, :, k] = (acc[b, half, :, 1, part_of(x), k] + rx1[0, b, half, :, :, k]) + (rx1[1, b, half, :, :, k] + rx1[2, b, half, :, :, k])
        for d in (1, 3, 2):
            second[b, h, "x", d].start()

    lasts = []

    def sum_second(b, h):
        for d in (1, 2, 3):
            second[b, h, "z", d].wait_recv()
            second[b, h, "x", d].wait_recv()
        k = pl.ds(256 * h, 256)
        for half in range(2):
            done[b, half, 0, :, k] = (sz[b, half, part_of(x), k] + rz2[0, b, half, :, k]) + (rz2[1, b, half, :, k] + rz2[2, b, half, :, k])
            done[b, half, 1, :, k] = (sx[b, half, z, :, k] + rx2[0, b, half, :, k]) + (rx2[1, b, half, :, k] + rx2[2, b, half, :, k])
        q = (y, y_t)[b]
        s = sems.take()[0]
        block = lambda: done.at[b, :, :, :, k]
        go = lambda: pltpu.make_async_remote_copy(src_ref=block(), dst_ref=fin.at[:, :, x], send_sem=s, recv_sem=recv.at[N_SEMS - 4 + x], device_id=dev(q, z, (y, y_l)[h], c), device_id_type=MESH)
        if h == 0:
            go = Copy((q != x, go))
            stay = Copy((q == x, lambda: pltpu.make_async_copy(block(), fin.at[:, :, x], local.at[12])))
            stay.start()
        else:
            go, stay = Copy((None, go)), Copy()
        go.start()
        lasts.append((go, stay))

    sum_first(0, 0)
    sum_first(0, 1)
    sum_first(1, 0)
    sum_first(1, 1)
    over_plane = share(ip, pair, at_plane, total(ig, over_group, 8))
    sum_second(0, 0)
    sum_second(0, 1)
    sum_second(1, 0)
    sum_second(1, 1)

    every = total(ip, over_plane, 16)
    matrix = jnp.concatenate([every[:, 32 * k : 32 * k + 32] for k in range(4)], axis=0)
    pairs.wait()
    first, kind = pair_list[0:1, :], pair_list[1:2, :]
    one_hot = (first == lax.broadcasted_iota(jnp.int32, (256, NP), 0)).astype(F32)
    kind = (kind == lax.broadcasted_iota(jnp.int32, (NP, NP), 0)).astype(F32)
    same_k = lax.dot_general(kind, kind, (((0,), (0,)), ((), ())), preferred_element_type=F32)
    highest = lax.Precision.HIGHEST
    outer = lax.dot_general(one_hot, same_k * matrix, (((1,), (0,)), ((), ())), precision=highest, preferred_element_type=F32)
    occ_ref[...] = -lax.dot_general(outer, one_hot, NT, precision=highest, preferred_element_type=F32)[:OCC]

    for go, stay in lasts:
        stay.wait()
    in_plane = (x == y) | (x == y_t)
    for q in range(4):
        came = Copy((jnp.logical_not(in_plane & (x == q)), lambda q=q: pltpu.make_async_remote_copy(src_ref=fin.at[:, :, q], dst_ref=fin.at[:, :, q], send_sem=send.at[0], recv_sem=recv.at[N_SEMS - 4 + q], device_id=to_l, device_id_type=MESH)))
        came.wait_recv()

    sent = y_lambda + y_amps + forward + core_amps + hop_l + hop_t + list(second_l.values()) + list(second_t.values())
    for group in (hop_s, more_l, more_t):
        sent += list(group.values())
    sent += [copy for when in firsts.values() for one in when for copy in one] + list(second.values()) + [go for go, _ in lasts] + over_group + over_plane
    for copy in sent:
        copy.wait_send()


def finish(fin_ref, occ_in, virt_ref, occ_ref):
    virt_ref[...] = fin_ref[...].reshape(128, 256).T[:ROWS, :120]
    occ_ref[...] = occ_in[:, :OCC]


def shards(lambda_blocks, amplitudes, pair_list):
    vmem = lambda shape, dtype=F32: pltpu.VMEM(shape, dtype)
    fin, occ = pl.pallas_call(
        kernel,
        out_shape=(jax.ShapeDtypeStruct((2, 2, 4, 8, 256), F32), jax.ShapeDtypeStruct((OCC, 256), F32)),
        in_specs=[pl.BlockSpec(memory_space=pl.ANY)] * 4,
        out_specs=(pl.BlockSpec(memory_space=pl.ANY), pl.BlockSpec(memory_space=pltpu.VMEM)),
        scratch_shapes=[
            vmem((2, 2, PAD, V)), vmem((4, 2, 2, 128, V)), vmem((512, 3 * KC), BF16), vmem((1024, 3 * KC), BF16), vmem((2, 2, 4, 2, 32, 512)),
            vmem((3, 2, 64, V)), vmem((3, 2, ROWS, 512)), vmem((4, 4, 2, 64, 512)), vmem((4, 4, 2, 64, 512)), vmem((256, 256)),
            vmem((3, 2, 2, 32, 512)), vmem((3, 2, 2, 4, 8, 512)), vmem((3, 2, 2, 8, 512)), vmem((3, 2, 2, 8, 512)),
            vmem((2, 2, 32, 512)), vmem((2, 2, 4, 8, 512)), vmem((2, 2, 2, 8, 512)), vmem((8, 8, 128)), vmem((16, 8, 128)), vmem((2, NP), jnp.int32),
            pltpu.SemaphoreType.DMA((N_SEMS,)), pltpu.SemaphoreType.DMA((N_SEMS,)), pltpu.SemaphoreType.DMA((22,)),
        ],
        compiler_params=pltpu.CompilerParams(collective_id=0, has_side_effects=True, vmem_limit_bytes=60 * 2**20),
        cost_estimate=pl.CostEstimate(flops=12_000_000_000, bytes_accessed=8_000_000, transcendentals=0),
    )(lambda_blocks, amplitudes, amplitudes.reshape(2, 2, 120, V), pair_list.T)
    return pl.pallas_call(
        finish,
        out_shape=(jax.ShapeDtypeStruct((ROWS, 120), F32), jax.ShapeDtypeStruct((OCC, OCC), F32)),
        in_specs=[pl.BlockSpec(memory_space=pltpu.VMEM)] * 2,
        out_specs=(pl.BlockSpec(memory_space=pltpu.VMEM),) * 2,
    )(fin, occ)


def solution(mesh):
    in_specs = (P("pair", "virt", None), P("pair", "virt", None), P())
    out_specs = (P("virt", "pair"), P())
    return jax.shard_map(shards, mesh=mesh, in_specs=in_specs, out_specs=out_specs, check_vma=False)
```
